32 devices in a mesh: rays: 8 (over y, x, core), planes: 4 (over z).
Axes of the slice: x: 2, y: 2, z: 4, core: 2. Of those that a mesh axis runs over, the one named last changes fastest.
Arguments:
- tile_density: bfloat16 [4, 256, 128, 128], P(None, 'rays', 'planes'), may hold values from -6 to 6
- long_maps: bfloat16 [8, 4, 512, 2, 512], P('rays'), may hold values from -1.796875 to 1.796875
- map_owner: int32 [4], replicated, may hold values from 0 to 7
- tile_lists: int32 [8, 4, 64], replicated, may hold values from 0 to 255, as said below
- block_slots: int32 [4, 512], P(None, ('rays', 'planes')), may hold values from 0 to 63
- block_windows: int32 [4, 2, 512], P(None, None, ('rays', 'planes')), may hold values from 0 to 384
- fine_cells: int32 [4, 2, 262144], P(None, None, ('rays', 'planes')), may hold values from 0 to 126
- long_cells: int32 [4, 2, 262144], P(None, None, ('rays', 'planes')), may hold values from 0 to 126
- fractions: float32 [4, 4, 262144], P(None, None, ('rays', 'planes')), may hold values from 0 to 1
Outputs:
- deflection: float32 [4, 2, 262144], P(None, None, ('rays', 'planes'))
- source_shift: float32 [2, 262144], P(None, ('rays', 'planes'))
The draws below stay inside these ranges and needn't reach their ends.
Inputs may be any that keep to these rules, and one draw needn't show every extreme that they name: `tile_lists`: tile t belongs to owner t // 32. In each list of one bundle and plane at most 16 entries name tiles of one owner, and some owner has exactly 16 entries in every such list; entries may repeat.
All inputs are finite; a program needn't handle non-finite values.
Results may differ from the reference program's by a relative error of at most 0.0064.
Values may be sent and summed in bfloat16 or wider, within the bound.
A program may use at most 128 MiB of HBM per device.

```python
import jax
import jax.numpy as jnp
from jax import lax

TS = 128
M = 512
PLANES = 4
TILES = 256
LIST = 64
RAYS_DEV = 8192
BLK = 512
RATIO = 16
TILE_DEV = 32
CAP = 16
RAYS = 262144
NBLK = 512
N_RAYS = 8
N_PLANES = 4


def draw_tile_lists(key, part):
    slot_count = N_RAYS * CAP

    def draw_single(single_key, flat_index):
        key_order, key_shuffle, key_local = jax.random.split(single_key, 3)
        shuffled = jax.random.permutation(key_order, slot_count)
        position = jnp.argsort(shuffled, stable=True).astype(jnp.int32)
        owner_ids = jnp.arange(slot_count, dtype=jnp.int32) // CAP
        bundle = flat_index // PLANES
        plane_index = flat_index % PLANES
        target = (bundle * 5 + plane_index * 3) % N_RAYS
        scores = position + jnp.where(owner_ids == target, 0, slot_count)
        chosen = jnp.argsort(scores, stable=True)[:LIST].astype(jnp.int32)
        chosen = jax.random.permutation(key_shuffle, chosen)
        local_index = jax.random.randint(key_local, (LIST,), 0, TILE_DEV, dtype=jnp.int32)
        return chosen // CAP * TILE_DEV + local_index
    key_list = jax.random.split(key, N_RAYS * PLANES)
    drawn = jax.vmap(draw_single)(key_list, jnp.arange(N_RAYS * PLANES, dtype=jnp.int32))
    return drawn.reshape(N_RAYS, PLANES, LIST).astype(jnp.int32)


def with_ends(values, own_key, low, top_value):
    extent = values.shape
    place = [jax.random.randint(jax.random.fold_in(own_key, axis), (), 0, extent[axis]) for axis in range(len(extent))]
    values = values.at[tuple(place)].set(low)
    longest = extent.index(max(extent))
    place[longest] = (place[longest] + 1) % extent[longest]
    return values.at[tuple(place)].set(top_value)


def steps_of(own_key, dims, pieces, low, top_value):
    level = 1.0
    for dim, parts in pieces:
        steps = jax.random.uniform(jax.random.fold_in(jax.random.fold_in(own_key, 6), dim), (parts,), jnp.float32, low / len(pieces), top_value / len(pieces))
        level = level * jnp.repeat(jnp.exp(steps), dims[dim] // parts).reshape((-1,) + (1,) * (len(dims) - 1 - dim))
    return level


def centred(stream_key, dims, spread, most, shards=(), kind=jnp.bfloat16):
    result = jax.random.normal(stream_key, dims, jnp.float32) * spread
    if len(shards) > 0:
        result = steps_of(stream_key, dims, shards, -0.22, 0.18) * result
    return jnp.clip(result, min=-most, max=most).astype(kind)


def setup_inputs(seed: int = 0) -> dict:
    streams_of = jax.random.split(jax.random.key(seed), 10)
    tile_density = centred(streams_of[0], (PLANES, TILES, TS, TS), 1.0, 6.0, ((1, 8), (2, 4)))
    long_maps = centred(streams_of[1], (N_RAYS, PLANES, M, 2, M), 0.3, 1.796875, ((0, 8),))
    map_owner = with_ends(jax.random.randint(streams_of[2], (PLANES,), 0, N_RAYS), jax.random.fold_in(streams_of[2], 1), 0, N_RAYS - 1).astype(jnp.int32)
    tile_lists = draw_tile_lists(jax.random.fold_in(streams_of[9], 71), 0)
    block_slots = with_ends(jax.random.randint(streams_of[4], (PLANES, NBLK), 0, LIST), jax.random.fold_in(streams_of[4], 1), 0, LIST - 1).astype(jnp.int32)
    block_windows = with_ends(jax.random.randint(streams_of[5], (PLANES, 2, NBLK), 0, M - TS + 1), jax.random.fold_in(streams_of[5], 1), 0, M - TS).astype(jnp.int32)
    fine_cells = with_ends(jax.random.randint(streams_of[6], (PLANES, 2, RAYS), 0, TS - 1), jax.random.fold_in(streams_of[6], 1), 0, (TS - 1) - 1).astype(jnp.int32)
    long_cells = with_ends(jax.random.randint(streams_of[7], (PLANES, 2, RAYS), 0, TS - 1), jax.random.fold_in(streams_of[7], 1), 0, (TS - 1) - 1).astype(jnp.int32)
    fractions = jnp.clip(1.0 * jax.random.uniform(streams_of[8], (PLANES, 4, RAYS), jnp.float32) ** steps_of(streams_of[8], (PLANES, 4, RAYS), ((2, 32),), -0.2, 0.2), 0.0, 1.0)
    return dict(tile_density=tile_density, long_maps=long_maps, map_owner=map_owner, tile_lists=tile_lists, block_slots=block_slots, block_windows=block_windows, fine_cells=fine_cells, long_cells=long_cells, fractions=fractions)


def kernel_tables(side):
    indices = jnp.arange(side, dtype=jnp.int32)
    offset = (indices[:, None] - indices[None, :]).astype(jnp.float32)
    tap_offsets = jnp.arange(-6, 7, dtype=jnp.int32).astype(jnp.float32)
    tap_total = jnp.sum(jnp.exp(-tap_offsets * tap_offsets / 8.0))
    inside = jnp.abs(offset) <= 6.0
    weight = jnp.where(inside, jnp.exp(-offset * offset / 8.0), 0.0) / tap_total
    smooth_table = weight.astype(jnp.bfloat16)
    slope_table = (6.0 * offset * weight / 4.0).astype(jnp.bfloat16)
    return smooth_table, slope_table


def rounded(values):
    return lax.optimization_barrier(values.astype(jnp.bfloat16)).astype(jnp.float32)


def convolve(density, smooth_table, slope_table):
    side = density.shape[1]
    right_table = jnp.concatenate([smooth_table.T, slope_table.T], axis=1).astype(jnp.float32)
    partial_value = rounded(jnp.einsum("lij,jk->lik", density.astype(jnp.float32), right_table))
    along_rows = jnp.einsum("ij,ljk->lik", slope_table.astype(jnp.float32), partial_value[:, :, :side])
    along_cols = jnp.einsum("ij,ljk->lik", smooth_table.astype(jnp.float32), partial_value[:, :, side:])
    return jnp.concatenate([along_rows, along_cols], axis=2).astype(jnp.bfloat16)


def interpolate(lookup, cell_row, cell_col, frac_row, frac_col):
    side = lookup.shape[1]
    positions = jnp.arange(side, dtype=jnp.int32)
    row_weight = jnp.where(positions == cell_row[..., None], 1.0 - frac_row[..., None], 0.0)
    row_weight = row_weight + jnp.where(positions == cell_row[..., None] + 1, frac_row[..., None], 0.0)
    col_weight = jnp.where(positions == cell_col[..., None], 1.0 - frac_col[..., None], 0.0)
    col_weight = col_weight + jnp.where(positions == cell_col[..., None] + 1, frac_col[..., None], 0.0)
    row_values = jnp.einsum("bns,bsk->bnk", rounded(row_weight), lookup.astype(jnp.float32))
    along_x = jnp.sum(row_values[..., :side] * col_weight, axis=-1)
    along_y = jnp.sum(row_values[..., side:] * col_weight, axis=-1)
    return along_x, along_y


def map_windows(map_full, starts, side):
    def one_window(row_start, col_start):
        window = lax.dynamic_slice(map_full, (row_start, jnp.int32(0), col_start), (side, 2, side))
        return window.reshape(side, 2 * side)
    return jax.vmap(one_window)(starts[0], starts[1])


def lens_shift(previous, target, template):
    shifts = jnp.zeros_like(template)
    for earlier_plane, deflect in enumerate(previous[:target]):
        shifts = shifts - ((target - earlier_plane) / target) * deflect
    return shifts


def plane_step(fine_lookup, long_lookup, fine_cell, long_cell, offsets, shifts):
    fine_x, fine_y = interpolate(fine_lookup, fine_cell[0], fine_cell[1], offsets[0] + shifts[0], offsets[1] + shifts[1])
    long_x, long_y = interpolate(long_lookup, long_cell[0], long_cell[1], offsets[2] + shifts[0] / RATIO, offsets[3] + shifts[1] / RATIO)
    return jnp.stack([fine_x + long_x, fine_y + long_y])


def reference(tile_density, long_maps, map_owner, tile_lists, block_slots, block_windows, fine_cells, long_cells, fractions):
    smooth_table, slope_table = kernel_tables(TS)
    all_fields = jnp.stack([convolve(tile_density[plane_index], smooth_table, slope_table) for plane_index in range(PLANES)])
    used_maps = jnp.stack([lax.dynamic_index_in_dim(long_maps[:, plane_index], map_owner[plane_index], 0, keepdims=False) for plane_index in range(PLANES)])
    groups = N_RAYS * N_PLANES
    blocks = RAYS_DEV // BLK

    def regroup(values):
        return jnp.moveaxis(values.reshape(PLANES, values.shape[1], groups, blocks, BLK), 2, 0)

    slots_grouped = jnp.moveaxis(block_slots.reshape(PLANES, groups, blocks), 1, 0)
    windows_grouped = jnp.moveaxis(block_windows.reshape(PLANES, 2, groups, blocks), 2, 0)

    def trace_group(inputs):
        group_index, slot_ids, window_starts, fine_group, long_group, frac_group = inputs
        bundle_lists = lax.dynamic_index_in_dim(tile_lists, group_index // N_PLANES, 0, keepdims=False)
        deflection_list = []
        for plane_index in range(PLANES):
            tile_ids = jnp.take(bundle_lists[plane_index], slot_ids[plane_index], axis=0)
            fine_lookup = jnp.take(all_fields[plane_index], tile_ids, axis=0)
            long_lookup = map_windows(used_maps[plane_index], window_starts[plane_index], TS)
            template = frac_group[plane_index][:2]
            shifts = lens_shift(deflection_list, plane_index, template)
            deflection_list.append(plane_step(fine_lookup, long_lookup, fine_group[plane_index], long_group[plane_index], frac_group[plane_index], shifts))
        source = lens_shift(deflection_list, PLANES, frac_group[0][:2])
        return jnp.stack(deflection_list), source

    deflect_all, source_all = lax.map(trace_group, (jnp.arange(groups, dtype=jnp.int32), slots_grouped, windows_grouped, regroup(fine_cells), regroup(long_cells), regroup(fractions)))
    deflection = jnp.moveaxis(deflect_all, 0, 2).reshape(PLANES, 2, RAYS)
    source_shift = jnp.moveaxis(source_all, 0, 1).reshape(2, RAYS)
    return deflection, source_shift
```

```python
import functools

import jax
import jax.numpy as jnp
import numpy as np
from jax import lax
from jax.experimental import pallas as pl
from jax.experimental.pallas import tpu as pltpu
from jax.sharding import PartitionSpec as P

RATIO = 16
ROW_ALIGN = 16
COL_ALIGN = 128


def kernel_tables(side):
    indices = np.arange(side)
    offset = (indices[:, None] - indices[None, :]).astype(np.float32)
    taps = np.arange(-6, 7).astype(np.float32)
    total = np.sum(np.exp(-taps * taps / np.float32(8.0)))
    inside = np.abs(offset) <= 6.0
    weight = np.where(inside, np.exp(-offset * offset / np.float32(8.0)), np.float32(0.0)) / total
    smooth = weight.astype(jnp.bfloat16)
    slope = (np.float32(6.0) * offset * weight / np.float32(4.0)).astype(jnp.bfloat16)
    return np.concatenate([smooth, slope], axis=0)


def dot_nt(a, b):
    return lax.dot_general(a, b, (((1,), (1,)), ((), ())), preferred_element_type=jnp.float32)


def hat(positions, cell, frac):
    return jnp.where(
        positions == cell, 1.0 - frac, jnp.where(positions == cell + 1, frac, 0.0)
    )


def look_up(table, row_cell, col_cell, row_frac, col_frac):
    side = table.shape[0] // 2
    width = row_cell.shape[1]
    rows = lax.broadcasted_iota(jnp.int32, (table.shape[1], width), 0)
    cols = lax.broadcasted_iota(jnp.int32, (side, width), 0)
    row_weight = hat(rows, row_cell, row_frac).astype(jnp.bfloat16)
    col_weight = hat(cols, col_cell, col_frac)
    values = jnp.dot(table, row_weight, preferred_element_type=jnp.float32)
    along_x = jnp.sum(values[:side] * col_weight, axis=0, keepdims=True)
    along_y = jnp.sum(values[side:] * col_weight, axis=0, keepdims=True)
    return along_x, along_y


def tile_fields(tile, tables):
    side = tile.shape[0]
    part = dot_nt(tables, tile).astype(jnp.bfloat16)
    along_x = dot_nt(part[:side], tables[side:])
    along_y = dot_nt(part[side:], tables[:side])
    return jnp.concatenate([along_x, along_y], axis=0).astype(jnp.bfloat16)


def map_window(read, row_start, col_start, side, map_side):
    rows = min(side + ROW_ALIGN, map_side)
    cols = min(side + COL_ALIGN, map_side)
    row_base = jnp.minimum(row_start // ROW_ALIGN * ROW_ALIGN, map_side - rows)
    col_base = jnp.minimum(col_start // COL_ALIGN * COL_ALIGN, map_side - cols)
    row_base = pl.multiple_of(row_base, ROW_ALIGN)
    col_base = pl.multiple_of(col_base, COL_ALIGN)
    here = lax.broadcasted_iota(jnp.int32, (side, cols), 0)
    there = lax.broadcasted_iota(jnp.int32, (side, cols), 1)
    pick = (there == here + (col_start - col_base)).astype(jnp.float32).astype(jnp.bfloat16)
    along_x = dot_nt(pick, read(0, pl.ds(row_base, rows), pl.ds(col_base, cols)))
    along_y = dot_nt(pick, read(1, pl.ds(row_base, rows), pl.ds(col_base, cols)))
    table = jnp.concatenate([along_x, along_y], axis=0).astype(jnp.bfloat16)
    return table, row_start - row_base


def plane_kernel(plane, last, windows, tables, strips, used, fine, long, fractions, *rest):
    previous, outs = rest[:plane], rest[plane:]
    block = pl.program_id(0)
    side = strips.shape[2]
    tile = strips[...].reshape(side, side)
    fields = tile_fields(tile, tables[...])
    window, row_extra = map_window(
        lambda c, r, s: used[c, r, s],
        windows[0, block],
        windows[1, block],
        side,
        used.shape[1],
    )
    shift_x = jnp.zeros_like(fractions[0:1, :])
    shift_y = shift_x
    for j, earlier in enumerate(previous):
        shift_x = shift_x - ((plane - j) / plane) * earlier[0:1, :]
        shift_y = shift_y - ((plane - j) / plane) * earlier[1:2, :]
    fine_x, fine_y = look_up(
        fields,
        fine[0:1, :],
        fine[1:2, :],
        fractions[0:1, :] + shift_x,
        fractions[1:2, :] + shift_y,
    )
    long_x, long_y = look_up(
        window,
        long[0:1, :] + row_extra,
        long[1:2, :],
        fractions[2:3, :] + shift_x / RATIO,
        fractions[3:4, :] + shift_y / RATIO,
    )
    value = jnp.concatenate([fine_x + long_x, fine_y + long_y], axis=0)
    outs[0][...] = value
    if last:
        count = plane + 1
        source = jnp.zeros_like(value)
        for j, earlier in enumerate(previous):
            source = source - ((count - j) / count) * earlier[...]
        outs[1][...] = source - (1 / count) * value


def run_plane(plane, last, windows, tables, strips, used, fine, long, fractions, previous):
    blocks = windows.shape[1]
    rays_here = fine.shape[1]
    width = rays_here // blocks
    rows = lambda n: pl.BlockSpec((n, width), lambda b: (0, b))
    whole = lambda x: pl.BlockSpec(x.shape, lambda b: (0,) * x.ndim)
    shape = jax.ShapeDtypeStruct((2, rays_here), jnp.float32)
    out_count = 2 if last else 1
    return pl.pallas_call(
        functools.partial(plane_kernel, plane, last),
        grid=(blocks,),
        out_shape=[shape] * out_count,
        in_specs=[
            pl.BlockSpec(memory_space=pltpu.SMEM),
            whole(tables),
            pl.BlockSpec((strips.shape[0], None, strips.shape[2], strips.shape[3]), lambda b: (0, b, 0, 0)),
            whole(used),
            rows(2),
            rows(2),
            rows(4),
        ]
        + [rows(2)] * plane,
        out_specs=[rows(2)] * out_count,
        compiler_params=pltpu.CompilerParams(vmem_limit_bytes=40 * 1024 * 1024),
        cost_estimate=pl.CostEstimate(
            flops=6 * rays_here * 128 * 256, bytes_accessed=4 << 20, transcendentals=0
        ),
    )(windows, tables, strips, used, fine, long, fractions, *previous)


def per_device(
    tile_density,
    long_maps,
    map_owner,
    tile_lists,
    block_slots,
    block_windows,
    fine_cells,
    long_cells,
    fractions,
):
    my_row = lax.axis_index("rays")
    strip_count = lax.axis_size("planes")
    plane_count, _, _, side = tile_density.shape
    tables = jnp.asarray(kernel_tables(side))
    blocks = block_slots.shape[1]

    slots = lax.all_gather(block_slots, "planes", axis=0)
    lists = lax.dynamic_index_in_dim(tile_lists, my_row, 0, keepdims=False)
    wanted = jnp.take_along_axis(lists[None], slots, axis=2)
    mine = (map_owner == my_row)[:, None, None, None]

    deflection = []
    for plane in range(plane_count):
        every = lax.all_gather(tile_density[plane], "rays", axis=0, tiled=True)
        out = jnp.take(every, wanted[:, plane].reshape(-1), axis=0, mode="clip")
        out = out.reshape((strip_count, blocks) + every.shape[1:])
        strips = lax.all_to_all(out, "planes", split_axis=0, concat_axis=0, tiled=True)
        own = jnp.transpose(long_maps[0, plane], (1, 0, 2))
        used = lax.psum(jnp.where(mine[plane], own, jnp.zeros_like(own)), "rays")
        result = run_plane(
            plane,
            plane == plane_count - 1,
            block_windows[plane],
            tables,
            strips,
            used,
            fine_cells[plane],
            long_cells[plane],
            fractions[plane],
            deflection,
        )
        deflection.append(result[0])
    return jnp.stack(deflection), result[1]


def solution(mesh):
    return jax.shard_map(
        per_device,
        mesh=mesh,
        in_specs=(
            P(None, "rays", "planes", None),
            P("rays", None, None, None, None),
            P(),
            P(),
            P(None, ("rays", "planes")),
            P(None, None, ("rays", "planes")),
            P(None, None, ("rays", "planes")),
            P(None, None, ("rays", "planes")),
            P(None, None, ("rays", "planes")),
        ),
        out_specs=(P(None, None, ("rays", "planes")), P(None, ("rays", "planes"))),
        check_vma=False,
    )
```

```python
import functools

import jax
import jax.numpy as jnp
import numpy as np
from jax import lax
from jax.experimental import pallas as pl
from jax.experimental.pallas import tpu as pltpu
from jax.sharding import PartitionSpec as P

RATIO = 16
ROW_ALIGN = 16
COL_ALIGN = 128


def kernel_tables(side):
    indices = np.arange(side)
    offset = (indices[:, None] - indices[None, :]).astype(np.float32)
    taps = np.arange(-6, 7).astype(np.float32)
    total = np.sum(np.exp(-taps * taps / np.float32(8.0)))
    inside = np.abs(offset) <= 6.0
    weight = np.where(inside, np.exp(-offset * offset / np.float32(8.0)), np.float32(0.0)) / total
    smooth = weight.astype(jnp.bfloat16)
    slope = (np.float32(6.0) * offset * weight / np.float32(4.0)).astype(jnp.bfloat16)
    return np.concatenate([smooth, slope], axis=0)


def dot_nt(a, b):
    return lax.dot_general(a, b, (((1,), (1,)), ((), ())), preferred_element_type=jnp.float32)


def hat(positions, cell, frac):
    return jnp.where(
        positions == cell, 1.0 - frac, jnp.where(positions == cell + 1, frac, 0.0)
    )


def look_up(table, row_cell, col_cell, row_frac, col_frac):
    side = table.shape[0] // 2
    width = row_cell.shape[1]
    rows = lax.broadcasted_iota(jnp.int32, (table.shape[1], width), 0)
    cols = lax.broadcasted_iota(jnp.int32, (side, width), 0)
    row_weight = hat(rows, row_cell, row_frac).astype(jnp.bfloat16)
    col_weight = hat(cols, col_cell, col_frac)
    values = jnp.dot(table, row_weight, preferred_element_type=jnp.float32)
    along_x = jnp.sum(values[:side] * col_weight, axis=0, keepdims=True)
    along_y = jnp.sum(values[side:] * col_weight, axis=0, keepdims=True)
    return along_x, along_y


def tile_fields(tile, tables):
    side = tile.shape[0]
    part = dot_nt(tables, tile).astype(jnp.bfloat16)
    along_x = dot_nt(part[:side], tables[side:])
    along_y = dot_nt(part[side:], tables[:side])
    return jnp.concatenate([along_x, along_y], axis=0).astype(jnp.bfloat16)


def map_window(along_x, along_y, col_extra, side):
    cols = along_x.shape[1]
    here = lax.broadcasted_iota(jnp.int32, (side, cols), 0)
    there = lax.broadcasted_iota(jnp.int32, (side, cols), 1)
    pick = (there == here + col_extra).astype(jnp.float32).astype(jnp.bfloat16)
    return jnp.concatenate(
        [dot_nt(pick, along_x), dot_nt(pick, along_y)], axis=0
    ).astype(jnp.bfloat16)


def flipped(value, bit):
    return value + (1 - 2 * (value // (1 << bit) % 2)) * (1 << bit)


def routes(count):
    levels = count.bit_length() - 1
    return list(range(1, levels)) + [0], list(range(levels - 1, 0, -1)) + [0]


def place(owner, order):
    return sum((owner // (1 << b) % 2) * (1 << i) for i, b in enumerate(order))


class Copies:
    def __init__(self, send, recv):
        self.send, self.recv, self.used, self.started = send, recv, 0, []

    def start(self, src, dst, device):
        i = self.used
        self.used += 1
        copy = pltpu.make_async_remote_copy(
            src_ref=src,
            dst_ref=dst,
            send_sem=self.send.at[i],
            recv_sem=self.recv.at[i],
            device_id=device,
            device_id_type=pl.DeviceIdType.MESH,
        )
        copy.start()
        self.started.append(copy)
        return copy


def copy_counts(n, nz, planes):
    levels = n.bit_length() - 1
    remote = (nz - 1) + planes * (2 * levels + (nz - 1) + 2 + 4 * (levels - 1))
    return remote, 3 * planes + nz


def body(
    n,
    nz,
    windows,
    spots,
    tables,
    density,
    maps,
    fine,
    long,
    fractions,
    deflection,
    source,
    every,
    out_strips,
    strips,
    used,
    full,
    landed,
    spots_all,
    spots_flat,
    send,
    recv,
    local,
):
    me, mz = lax.axis_index("rays"), lax.axis_index("planes")
    planes, tiles_here = density.shape[0], density.shape[1]
    part = tiles_here // 2
    levels = n.bit_length() - 1
    orders = routes(n)
    core = me % 2
    rows = used.shape[1]
    half = rows // 2
    blocks = windows.shape[2]
    side = tables.shape[1]
    width = fine.shape[2] // blocks
    keep = pl.multiple_of(core * half, ROW_ALIGN)
    away = pl.multiple_of((1 - core) * half, ROW_ALIGN)
    locals_used = [0]

    def local_copy(src, dst):
        copy = pltpu.make_async_copy(src, dst, local.at[locals_used[0]])
        locals_used[0] += 1
        copy.start()
        return copy

    def rays_peer(bit):
        return {"rays": flipped(me, bit), "planes": mz}

    def planes_peer(step):
        return {"rays": me, "planes": lax.rem(mz + step, nz)}

    own_spots = [place(me, order) for order in orders]
    fetched = []
    for k in range(planes):
        pair = []
        for h in range(2):
            at = (h * n + own_spots[h]) * part
            pair.append(
                local_copy(density.at[k, pl.ds(h * part, part)], every[k].at[pl.ds(at, part)])
            )
        pair.append(local_copy(maps.at[k, pl.ds(keep, half)], used.at[k, pl.ds(keep, half)]))
        fetched.append(pair)

    barrier = pltpu.get_barrier_semaphore()
    for bit in range(levels):
        pl.semaphore_signal(
            barrier, inc=1, device_id=rays_peer(bit), device_id_type=pl.DeviceIdType.MESH
        )
    for step in range(1, nz):
        pl.semaphore_signal(
            barrier, inc=1, device_id=planes_peer(step), device_id_type=pl.DeviceIdType.MESH
        )
    pl.semaphore_wait(barrier, levels + nz - 1)

    copies = Copies(send, recv)
    spot_copies = [
        copies.start(spots, spots_all.at[mz], planes_peer(step)) for step in range(1, nz)
    ]

    def spread_tiles(k):
        flight = []
        for i in range(levels):
            if i == 0:
                fetched[k][0].wait()
                fetched[k][1].wait()
            for copy in flight:
                copy.wait_recv()
            flight = []
            for h, order in enumerate(orders):
                base = own_spots[h] // (1 << i) * (1 << i)
                area = every[k].at[pl.ds((h * n + base) * part, part << i)]
                flight.append(copies.start(area, area, rays_peer(order[i])))
            yield
        for copy in flight:
            copy.wait_recv()
        if k == 0:
            for copy in spot_copies:
                copy.wait_recv()
            loads = [local_copy(spots, spots_flat.at[mz])]
            for step in range(1, nz):
                there = lax.rem(mz + step, nz)
                loads.append(local_copy(spots_all.at[there], spots_flat.at[there]))
            for load in loads:
                load.wait()
        flight = []
        for step in range(nz):
            there = lax.rem(mz + step, nz)

            def gather(b, carry):
                strip = every[k][spots_flat[there, k, b]]
                if step == 0:
                    strips[k, mz, b] = strip
                else:
                    out_strips[k, step - 1, b] = strip
                return carry

            lax.fori_loop(0, blocks, gather, 0)
            if step > 0:
                flight.append(
                    copies.start(out_strips.at[k, step - 1], strips.at[k, mz], planes_peer(step))
                )
        yield
        for copy in flight:
            copy.wait_recv()

    def spread_map(k):
        first = copies.start(maps.at[k, pl.ds(away, half)], landed.at[k, pl.ds(0, half)], rays_peer(0))
        yield
        first.wait_recv()
        fetched[k][2].wait()
        used[k, pl.ds(keep, half)] = used[k, pl.ds(keep, half)] + landed[k, pl.ds(0, half)]
        base = [core * half + h * (half // 2) for h in range(2)]
        spot = [half + h * (half // 2) for h in range(2)]
        size = half // 2
        paths = [order[:-1] for order in orders]
        for i in range(levels - 1):
            size //= 2
            flight = []
            for h in range(2):
                bit = me // (1 << paths[h][i]) % 2
                give = pl.multiple_of(base[h] + (1 - bit) * size, ROW_ALIGN)
                flight.append(
                    copies.start(
                        used.at[k, pl.ds(give, size)],
                        landed.at[k, pl.ds(spot[h], size)],
                        rays_peer(paths[h][i]),
                    )
                )
                base[h] = base[h] + bit * size
            yield
            for h in range(2):
                flight[h].wait_recv()
                at = pl.multiple_of(base[h], ROW_ALIGN)
                total = used[k, pl.ds(at, size)] + landed[k, pl.ds(spot[h], size)]
                if i < levels - 2:
                    used[k, pl.ds(at, size)] = total
                else:
                    full[k][pl.ds(at, size)] = total
                spot[h] += size
        for i in reversed(range(levels - 1)):
            flight = []
            for h in range(2):
                area = full[k].at[pl.ds(pl.multiple_of(base[h], ROW_ALIGN), size)]
                flight.append(copies.start(area, area, rays_peer(paths[h][i])))
                base[h] = base[h] - (me // (1 << paths[h][i]) % 2) * size
            yield
            size *= 2
            for copy in flight:
                copy.wait_recv()
        area = full[k].at[pl.ds(keep, half)]
        last = copies.start(area, area, rays_peer(0))
        yield
        last.wait_recv()

    chunks = map_side_chunks(rows, side)
    map_rows = rows // (2 * chunks)

    def compute(k):
        def one(b, carry):
            rays = pl.ds(pl.multiple_of(b * width, width), width)
            tile = strips[k, :, b].reshape(side, side)
            fields = tile_fields(tile, tables[...])

            span = side + ROW_ALIGN
            pieces = []
            for comp in range(2):
                pieces.append(
                    jnp.concatenate(
                        [
                            full[k][
                                pl.ds(
                                    windows[k, 0, b] * ROW_ALIGN + (comp * chunks + j) * map_rows,
                                    span,
                                )
                            ]
                            for j in range(2)
                        ],
                        axis=1,
                    )
                )
            window = map_window(pieces[0], pieces[1], windows[k, 2, b], side)
            row_extra = windows[k, 1, b]
            frac = fractions[k, :, rays]
            shift_x = jnp.zeros_like(frac[0:1])
            shift_y = shift_x
            for j in range(k):
                earlier = deflection[j, :, rays]
                shift_x = shift_x - ((k - j) / k) * earlier[0:1]
                shift_y = shift_y - ((k - j) / k) * earlier[1:2]
            fine_cell, long_cell = fine[k, :, rays], long[k, :, rays]
            fine_x, fine_y = look_up(
                fields, fine_cell[0:1], fine_cell[1:2], frac[0:1] + shift_x, frac[1:2] + shift_y
            )
            long_x, long_y = look_up(
                window,
                long_cell[0:1] + row_extra,
                long_cell[1:2],
                frac[2:3] + shift_x / RATIO,
                frac[3:4] + shift_y / RATIO,
            )
            value = jnp.concatenate([fine_x + long_x, fine_y + long_y], axis=0)
            deflection[k, :, rays] = value
            if k == planes - 1:
                total = jnp.zeros_like(value)
                for j in range(k):
                    total = total - ((planes - j) / planes) * deflection[j, :, rays]
                source[:, rays] = total - (1 / planes) * value
            return carry

        lax.fori_loop(0, blocks, one, 0)

    active = {}
    waiting = list(range(planes))
    while active or waiting:
        if waiting:
            k = waiting.pop(0)
            active[k] = [spread_tiles(k), spread_map(k)]
        ready = []
        for k in list(active):
            active[k] = [g for g in active[k] if next(g, True) is None]
            if not active[k]:
                del active[k]
                ready.append(k)
        for k in ready:
            compute(k)
    for copy in copies.started:
        copy.wait_send()


def map_side_chunks(rows, side):
    chunks = 1
    while 2 * chunks * chunks * side < rows:
        chunks += 1
    return chunks


def per_device(
    n,
    nz,
    tile_density,
    long_maps,
    map_owner,
    tile_lists,
    block_slots,
    block_windows,
    fine_cells,
    long_cells,
    fractions,
):
    my_row = lax.axis_index("rays")
    planes, tiles_here, strip_rows, side = tile_density.shape
    map_side = long_maps.shape[2]
    rays_here = fine_cells.shape[2]
    blocks = block_slots.shape[1]
    part = tiles_here // 2
    chunks = map_side // COL_ALIGN
    map_rows = 2 * chunks * map_side
    tables = jnp.asarray(kernel_tables(side))

    lists = lax.dynamic_index_in_dim(tile_lists, my_row, 0, keepdims=False)
    tiles = jnp.take_along_axis(lists, block_slots, axis=1)
    owner, inside = tiles // tiles_here, tiles % tiles_here
    order_a, order_b = routes(n)
    spot_a = place(owner, order_a) * part + inside
    spot_b = (n + place(owner, order_b)) * part + inside - part
    spots = jnp.where(inside < part, spot_a, spot_b)
    spots = jnp.pad(spots, ((0, 8 - planes), (0, 128 - blocks)))
    row_at, col_at = block_windows[:, 0], block_windows[:, 1]
    row_base = jnp.minimum(row_at // ROW_ALIGN, (map_side - side) // ROW_ALIGN - 1)
    col_base = jnp.minimum(col_at // COL_ALIGN, chunks - 2)
    windows = jnp.stack(
        [
            row_base + col_base * (map_side // ROW_ALIGN),
            row_at - row_base * ROW_ALIGN,
            col_at - col_base * COL_ALIGN,
        ],
        axis=1,
    )

    mine = (map_owner == my_row)[:, None, None, None, None]
    own = long_maps[0].reshape(planes, map_side, 2, chunks, COL_ALIGN)
    own = jnp.transpose(own, (0, 2, 3, 1, 4))
    own = jnp.where(mine, own, jnp.zeros_like(own)).reshape(planes, map_rows, COL_ALIGN)

    remote, local = copy_counts(n, nz, planes)
    vmem = pl.BlockSpec(memory_space=pltpu.VMEM)
    smem = pl.BlockSpec(memory_space=pltpu.SMEM)
    anywhere = pl.BlockSpec(memory_space=pl.ANY)
    kind = tile_density.dtype
    return pl.pallas_call(
        functools.partial(body, n, nz),
        out_shape=[
            jax.ShapeDtypeStruct((planes, 2, rays_here), jnp.float32),
            jax.ShapeDtypeStruct((2, rays_here), jnp.float32),
        ],
        in_specs=[smem, vmem, vmem, anywhere, anywhere, vmem, vmem, vmem],
        out_specs=[vmem, vmem],
        scratch_shapes=[
            [pltpu.VMEM((n * tiles_here, strip_rows, side), kind)] * planes,
            pltpu.VMEM((planes, nz - 1, blocks, strip_rows, side), kind),
            pltpu.VMEM((planes, nz, blocks, strip_rows, side), kind),
            pltpu.VMEM((planes, map_rows, COL_ALIGN), kind),
            [pltpu.VMEM((map_rows, COL_ALIGN), kind)] * planes,
            pltpu.VMEM((planes, map_rows, COL_ALIGN), kind),
            pltpu.VMEM((nz,) + spots.shape, jnp.int32),
            pltpu.SMEM((nz,) + spots.shape, jnp.int32),
            pltpu.SemaphoreType.DMA((remote,)),
            pltpu.SemaphoreType.DMA((remote,)),
            pltpu.SemaphoreType.DMA((local,)),
        ],
        compiler_params=pltpu.CompilerParams(
            collective_id=0, has_side_effects=True, vmem_limit_bytes=52 * 1024 * 1024
        ),
        cost_estimate=pl.CostEstimate(
            flops=6 * planes * rays_here * 128 * 256, bytes_accessed=16 << 20, transcendentals=0
        ),
    )(windows, spots, tables, tile_density, own, fine_cells, long_cells, fractions)


def solution(mesh):
    return jax.shard_map(
        functools.partial(per_device, mesh.shape["rays"], mesh.shape["planes"]),
        mesh=mesh,
        in_specs=(
            P(None, "rays", "planes", None),
            P("rays", None, None, None, None),
            P(),
            P(),
            P(None, ("rays", "planes")),
            P(None, None, ("rays", "planes")),
            P(None, None, ("rays", "planes")),
            P(None, None, ("rays", "planes")),
            P(None, None, ("rays", "planes")),
        ),
        out_specs=(P(None, None, ("rays", "planes")), P(None, ("rays", "planes"))),
        check_vma=False,
    )
```

```python
import functools

import jax
import jax.numpy as jnp
import numpy as np
from jax import lax
from jax.experimental import pallas as pl
from jax.experimental.pallas import tpu as pltpu
from jax.sharding import PartitionSpec as P

RATIO = 16
ROW_ALIGN = 16
COL_ALIGN = 128
TILE_GROUP = 4
MAP_GROUP = 4
RAY_GROUP = 2


def kernel_tables(side):
    indices = np.arange(side)
    offset = (indices[:, None] - indices[None, :]).astype(np.float32)
    taps = np.arange(-6, 7).astype(np.float32)
    total = np.sum(np.exp(-taps * taps / np.float32(8.0)))
    inside = np.abs(offset) <= 6.0
    weight = np.where(inside, np.exp(-offset * offset / np.float32(8.0)), np.float32(0.0)) / total
    smooth = weight.astype(jnp.bfloat16)
    slope = (np.float32(6.0) * offset * weight / np.float32(4.0)).astype(jnp.bfloat16)
    return np.concatenate([smooth, slope], axis=0)


def dot_nt(a, b):
    return lax.dot_general(a, b, (((1,), (1,)), ((), ())), preferred_element_type=jnp.float32)


def hat(positions, cell, frac):
    return jnp.where(
        positions == cell, 1.0 - frac, jnp.where(positions == cell + 1, frac, 0.0)
    )


def look_up(table, row_cell, col_cell, row_frac, col_frac):
    side = table.shape[0] // 2
    width = row_cell.shape[1]
    rows = lax.broadcasted_iota(jnp.int32, (table.shape[1], width), 0)
    cols = lax.broadcasted_iota(jnp.int32, (side, width), 0)
    row_weight = hat(rows, row_cell, row_frac).astype(jnp.bfloat16)
    col_weight = hat(cols, col_cell, col_frac)
    values = jnp.dot(table, row_weight, preferred_element_type=jnp.float32)
    along_x = jnp.sum(values[:side] * col_weight, axis=0, keepdims=True)
    along_y = jnp.sum(values[side:] * col_weight, axis=0, keepdims=True)
    return along_x, along_y


def tile_fields(tile, tables):
    side = tile.shape[0]
    part = dot_nt(tables, tile).astype(jnp.bfloat16)
    along_x = dot_nt(part[:side], tables[side:])
    along_y = dot_nt(part[side:], tables[:side])
    return jnp.concatenate([along_x, along_y], axis=0).astype(jnp.bfloat16)


def map_window(along_x, along_y, col_extra, side):
    cols = along_x.shape[1]
    here = lax.broadcasted_iota(jnp.int32, (side, cols), 0)
    there = lax.broadcasted_iota(jnp.int32, (side, cols), 1)
    pick = (there == here + col_extra).astype(jnp.float32).astype(jnp.bfloat16)
    return jnp.concatenate(
        [dot_nt(pick, along_x), dot_nt(pick, along_y)], axis=0
    ).astype(jnp.bfloat16)


def flipped(value, bit):
    return value + (1 - 2 * (value // (1 << bit) % 2)) * (1 << bit)


def routes(count):
    levels = count.bit_length() - 1
    return list(range(1, levels)) + [0], list(range(levels - 1, 0, -1)) + [0]


def place(owner, order):
    return sum((owner // (1 << b) % 2) * (1 << i) for i, b in enumerate(order))


class Copies:
    def __init__(self, send, recv):
        self.send, self.recv, self.used, self.started = send, recv, 0, []

    def start(self, src, dst, device):
        i = self.used
        self.used += 1
        copy = pltpu.make_async_remote_copy(
            src_ref=src,
            dst_ref=dst,
            send_sem=self.send.at[i],
            recv_sem=self.recv.at[i],
            device_id=device,
            device_id_type=pl.DeviceIdType.MESH,
        )
        copy.start()
        self.started.append(copy)
        return copy


def copy_counts(n, nz, planes):
    levels = n.bit_length() - 1
    remote = (nz - 1) + planes * (2 * levels + (nz - 1) + 2 + 4 * (levels - 1))
    return remote, 3 * planes + nz


def body(
    n,
    nz,
    windows,
    held,
    spots,
    tables,
    unmix,
    density,
    maps,
    fine,
    long,
    fractions,
    deflection,
    source,
    every,
    out_strips,
    strips,
    used,
    full,
    landed,
    planar,
    fields,
    spots_all,
    spots_flat,
    send,
    recv,
    local,
):
    me, mz = lax.axis_index("rays"), lax.axis_index("planes")
    planes, tiles_here = density.shape[0], density.shape[1]
    part = tiles_here // 2
    levels = n.bit_length() - 1
    orders = routes(n)
    core = me % 2
    rows = used.shape[1]
    half = rows // 2
    blocks = windows.shape[2]
    side = tables.shape[1]
    width = fine.shape[2] // blocks
    keep = pl.multiple_of(core * half, ROW_ALIGN)
    away = pl.multiple_of((1 - core) * half, ROW_ALIGN)
    locals_used = [0]

    def local_copy(src, dst):
        copy = pltpu.make_async_copy(src, dst, local.at[locals_used[0]])
        locals_used[0] += 1
        copy.start()
        return copy

    def rays_peer(bit):
        return {"rays": flipped(me, bit), "planes": mz}

    def planes_peer(step):
        return {"rays": me, "planes": lax.rem(mz + step, nz)}

    own_spots = [place(me, order) for order in orders]
    fetched = []
    for k in range(planes):
        pair = []
        for h in range(2):
            at = (h * n + own_spots[h]) * part
            pair.append(
                local_copy(density.at[k, pl.ds(h * part, part)], every[k].at[pl.ds(at, part)])
            )
        pair.append(local_copy(maps.at[k, pl.ds(keep, half)], used.at[k, pl.ds(keep, half)]))
        fetched.append(pair)

    barrier = pltpu.get_barrier_semaphore()
    for bit in range(levels):
        pl.semaphore_signal(
            barrier, inc=1, device_id=rays_peer(bit), device_id_type=pl.DeviceIdType.MESH
        )
    for step in range(1, nz):
        pl.semaphore_signal(
            barrier, inc=1, device_id=planes_peer(step), device_id_type=pl.DeviceIdType.MESH
        )
    pl.semaphore_wait(barrier, levels + nz - 1)

    copies = Copies(send, recv)
    spot_copies = [
        copies.start(spots, spots_all.at[mz], planes_peer(step)) for step in range(1, nz)
    ]

    def spread_tiles(k):
        flight = []
        for i in range(levels):
            if i == 0:
                fetched[k][0].wait()
                fetched[k][1].wait()
            for copy in flight:
                copy.wait_recv()
            flight = []
            for h, order in enumerate(orders):
                base = own_spots[h] // (1 << i) * (1 << i)
                area = every[k].at[pl.ds((h * n + base) * part, part << i)]
                flight.append(copies.start(area, area, rays_peer(order[i])))
            yield
        for copy in flight:
            copy.wait_recv()
        if k == 0:
            for copy in spot_copies:
                copy.wait_recv()
            loads = [local_copy(spots, spots_flat.at[mz])]
            for step in range(1, nz):
                there = lax.rem(mz + step, nz)
                loads.append(local_copy(spots_all.at[there], spots_flat.at[there]))
            for load in loads:
                load.wait()
        flight = []
        for step in range(nz):
            there = lax.rem(mz + step, nz)

            def gather(b, carry):
                strip = every[k][spots_flat[there, k, b]]
                if step == 0:
                    strips[k, mz, b] = strip
                else:
                    out_strips[k, step - 1, b] = strip
                return carry

            lax.fori_loop(0, blocks, gather, 0)
            if step > 0:
                flight.append(
                    copies.start(out_strips.at[k, step - 1], strips.at[k, mz], planes_peer(step))
                )
        yield
        for copy in flight:
            copy.wait_recv()

    def choose(mine, here, there):
        weight = jnp.full((1, here.shape[1]), mine, jnp.float32)
        return here * weight.astype(here.dtype) + there * (1.0 - weight).astype(here.dtype)

    def spread_map(k):
        first = copies.start(maps.at[k, pl.ds(away, half)], landed.at[k, pl.ds(0, half)], rays_peer(0))
        yield
        first.wait_recv()
        fetched[k][2].wait()
        used[k, pl.ds(keep, half)] = choose(
            held[k, 0, 0], used[k, pl.ds(keep, half)], landed[k, pl.ds(0, half)]
        )
        base = [core * half + h * (half // 2) for h in range(2)]
        spot = [half + h * (half // 2) for h in range(2)]
        size = half // 2
        paths = [order[:-1] for order in orders]
        for i in range(levels - 1):
            size //= 2
            flight = []
            for h in range(2):
                bit = me // (1 << paths[h][i]) % 2
                give = pl.multiple_of(base[h] + (1 - bit) * size, ROW_ALIGN)
                flight.append(
                    copies.start(
                        used.at[k, pl.ds(give, size)],
                        landed.at[k, pl.ds(spot[h], size)],
                        rays_peer(paths[h][i]),
                    )
                )
                base[h] = base[h] + bit * size
            yield
            for h in range(2):
                flight[h].wait_recv()
                at = pl.multiple_of(base[h], ROW_ALIGN)
                total = choose(
                    held[k, h, i + 1], used[k, pl.ds(at, size)], landed[k, pl.ds(spot[h], size)]
                )
                if i < levels - 2:
                    used[k, pl.ds(at, size)] = total
                else:
                    full[k][pl.ds(at, size)] = total
                spot[h] += size
        for i in reversed(range(levels - 1)):
            flight = []
            for h in range(2):
                area = full[k].at[pl.ds(pl.multiple_of(base[h], ROW_ALIGN), size)]
                flight.append(copies.start(area, area, rays_peer(paths[h][i])))
                base[h] = base[h] - (me // (1 << paths[h][i]) % 2) * size
            yield
            size *= 2
            for copy in flight:
                copy.wait_recv()
        area = full[k].at[pl.ds(keep, half)]
        last = copies.start(area, area, rays_peer(0))
        yield
        last.wait_recv()

    chunks = map_side_chunks(rows, side)
    map_rows = rows // (2 * chunks)

    def convolve_tiles(k):
        def some(g, carry):
            made = []
            for u in range(TILE_GROUP):
                tile = strips[k, :, g * TILE_GROUP + u].reshape(side, side)
                made.append(tile_fields(tile, tables[...]))
            for u in range(TILE_GROUP):
                fields[k, g * TILE_GROUP + u] = made[u]
            return carry

        lax.fori_loop(0, blocks // TILE_GROUP, some, 0)

    def separate(k):
        kinds = 2 * chunks
        span = side // kinds

        def some(g, carry):
            parts = []
            for u in range(MAP_GROUP):
                at = pl.multiple_of((g * MAP_GROUP + u) * side, side)
                parts.append(
                    jnp.dot(
                        unmix[...], full[k][pl.ds(at, side)], preferred_element_type=jnp.float32
                    ).astype(jnp.bfloat16)
                )
            moved = jnp.concatenate(
                [part.reshape(kinds, span, side) for part in parts], axis=1
            )
            at = pl.multiple_of(g * (MAP_GROUP * span), MAP_GROUP * span)
            for j in range(kinds):
                planar[k, pl.ds(j * map_rows + at, MAP_GROUP * span)] = moved[j]
            return carry

        lax.fori_loop(0, rows // (side * MAP_GROUP), some, 0)

    def look(k, b):
        rays = pl.ds(pl.multiple_of(b * width, width), width)
        span = side + ROW_ALIGN
        pieces = []
        for comp in range(2):
            lanes = []
            for j in range(2):
                at = windows[k, 0, b] * ROW_ALIGN + (2 * j + comp) * map_rows
                lanes.append(planar[k, pl.ds(at, span)])
            pieces.append(jnp.concatenate(lanes, axis=1))
        window = map_window(pieces[0], pieces[1], windows[k, 2, b], side)
        row_extra = windows[k, 1, b]
        frac = fractions[k, :, rays]
        shift = jnp.zeros_like(frac[0:2])
        for j in range(k):
            shift = shift - ((k - j) / k) * deflection[j, :, rays]
        shift_x, shift_y = shift[0:1], shift[1:2]
        fine_cell, long_cell = fine[k, :, rays], long[k, :, rays]
        fine_x, fine_y = look_up(
            fields[k, b], fine_cell[0:1], fine_cell[1:2], frac[0:1] + shift_x, frac[1:2] + shift_y
        )
        long_x, long_y = look_up(
            window,
            long_cell[0:1] + row_extra,
            long_cell[1:2],
            frac[2:3] + shift_x / RATIO,
            frac[3:4] + shift_y / RATIO,
        )
        value = jnp.concatenate([fine_x + long_x, fine_y + long_y], axis=0)
        total = jnp.zeros_like(value)
        if k == planes - 1:
            for j in range(k):
                total = total - ((planes - j) / planes) * deflection[j, :, rays]
            total = total - (1 / planes) * value
        return rays, value, total

    def compute(k):
        def some(g, carry):
            done = [look(k, g * RAY_GROUP + u) for u in range(RAY_GROUP)]
            for rays, value, total in done:
                deflection[k, :, rays] = value
                if k == planes - 1:
                    source[:, rays] = total
            return carry

        lax.fori_loop(0, blocks // RAY_GROUP, some, 0)

    active = {}
    waiting = list(range(planes))
    while active or waiting:
        if waiting:
            k = waiting.pop(0)
            active[k] = {convolve_tiles: spread_tiles(k), separate: spread_map(k)}
        ready = []
        for k in list(active):
            for after, steps in list(active[k].items()):
                if next(steps, True) is True:
                    del active[k][after]
                    ready.append((after, k))
            if not active[k]:
                del active[k]
                ready.append((compute, k))
        for after, k in ready:
            after(k)
    for copy in copies.started:
        copy.wait_send()


def map_side_chunks(rows, side):
    chunks = 1
    while 2 * chunks * chunks * side < rows:
        chunks += 1
    return chunks


def per_device(
    n,
    nz,
    tile_density,
    long_maps,
    map_owner,
    tile_lists,
    block_slots,
    block_windows,
    fine_cells,
    long_cells,
    fractions,
):
    my_row = lax.axis_index("rays")
    planes, tiles_here, strip_rows, side = tile_density.shape
    map_side = long_maps.shape[2]
    rays_here = fine_cells.shape[2]
    blocks = block_slots.shape[1]
    part = tiles_here // 2
    chunks = map_side // COL_ALIGN
    map_rows = 2 * chunks * map_side
    tables = jnp.asarray(kernel_tables(side))

    lists = lax.dynamic_index_in_dim(tile_lists, my_row, 0, keepdims=False)
    picked = block_slots[:, :, None] == jnp.arange(lists.shape[1], dtype=jnp.int32)
    tiles = jnp.sum(jnp.where(picked, lists[:, None, :], 0), axis=2)
    owner, inside = tiles // tiles_here, tiles % tiles_here
    order_a, order_b = routes(n)
    spot_a = place(owner, order_a) * part + inside
    spot_b = (n + place(owner, order_b)) * part + inside - part
    spots = jnp.where(inside < part, spot_a, spot_b)
    spots = jnp.pad(spots, ((0, 8 - planes), (0, 128 - blocks)))
    row_at, col_at = block_windows[:, 0], block_windows[:, 1]
    row_base = jnp.minimum(row_at // ROW_ALIGN, (map_side - side) // ROW_ALIGN - 1)
    col_base = jnp.minimum(col_at // COL_ALIGN, chunks - 2)
    windows = jnp.stack(
        [
            row_base + 2 * col_base * (map_side // ROW_ALIGN),
            row_at - row_base * ROW_ALIGN,
            col_at - col_base * COL_ALIGN,
        ],
        axis=1,
    )

    own = long_maps[0].reshape(planes, map_side, 2, chunks, COL_ALIGN)
    own = jnp.transpose(own, (0, 1, 3, 2, 4)).reshape(planes, map_rows, COL_ALIGN)
    unlike = map_owner[:, None, None] ^ my_row
    levels = n.bit_length() - 1
    reached = [
        [sum(1 << b for b in ([0] + order[:-1])[:i]) for i in range(levels)]
        for order in (order_a, order_b)
    ]
    apart = jnp.asarray([[n - 1 - r for r in row] for row in reached], jnp.int32)
    held = ((unlike & apart) == 0).astype(jnp.float32)
    kinds = 2 * chunks
    span = side // kinds
    to = np.arange(side)
    unmix = (to[None, :] == (to[:, None] % span) * kinds + to[:, None] // span).astype(jnp.bfloat16)

    remote, local = copy_counts(n, nz, planes)
    vmem = pl.BlockSpec(memory_space=pltpu.VMEM)
    smem = pl.BlockSpec(memory_space=pltpu.SMEM)
    anywhere = pl.BlockSpec(memory_space=pl.ANY)
    kind = tile_density.dtype
    return pl.pallas_call(
        functools.partial(body, n, nz),
        out_shape=[
            jax.ShapeDtypeStruct((planes, 2, rays_here), jnp.float32),
            jax.ShapeDtypeStruct((2, rays_here), jnp.float32),
        ],
        in_specs=[smem, smem, vmem, vmem, vmem, anywhere, anywhere, vmem, vmem, vmem],
        out_specs=[vmem, vmem],
        scratch_shapes=[
            [pltpu.VMEM((n * tiles_here, strip_rows, side), kind)] * planes,
            pltpu.VMEM((planes, nz - 1, blocks, strip_rows, side), kind),
            pltpu.VMEM((planes, nz, blocks, strip_rows, side), kind),
            pltpu.VMEM((planes, map_rows, COL_ALIGN), kind),
            [pltpu.VMEM((map_rows, COL_ALIGN), kind)] * planes,
            pltpu.VMEM((planes, map_rows, COL_ALIGN), kind),
            pltpu.VMEM((planes, map_rows, COL_ALIGN), kind),
            pltpu.VMEM((planes, blocks, 2 * side, side), kind),
            pltpu.VMEM((nz,) + spots.shape, jnp.int32),
            pltpu.SMEM((nz,) + spots.shape, jnp.int32),
            pltpu.SemaphoreType.DMA((remote,)),
            pltpu.SemaphoreType.DMA((remote,)),
            pltpu.SemaphoreType.DMA((local,)),
        ],
        compiler_params=pltpu.CompilerParams(
            collective_id=0, has_side_effects=True, vmem_limit_bytes=52 * 1024 * 1024
        ),
        cost_estimate=pl.CostEstimate(
            flops=6 * planes * rays_here * 128 * 256, bytes_accessed=16 << 20, transcendentals=0
        ),
    )(windows, held, spots, tables, jnp.asarray(unmix), tile_density, own, fine_cells, long_cells, fractions)


def solution(mesh):
    return jax.shard_map(
        functools.partial(per_device, mesh.shape["rays"], mesh.shape["planes"]),
        mesh=mesh,
        in_specs=(
            P(None, "rays", "planes", None),
            P("rays", None, None, None, None),
            P(),
            P(),
            P(None, ("rays", "planes")),
            P(None, None, ("rays", "planes")),
            P(None, None, ("rays", "planes")),
            P(None, None, ("rays", "planes")),
            P(None, None, ("rays", "planes")),
        ),
        out_specs=(P(None, None, ("rays", "planes")), P(None, ("rays", "planes"))),
        check_vma=False,
    )
```

```python
import functools

import jax
import jax.numpy as jnp
import numpy as np
from jax import lax
from jax.experimental import pallas as pl
from jax.experimental.pallas import tpu as pltpu
from jax.sharding import PartitionSpec as P

RATIO = 16
ROW_ALIGN = 16
COL_ALIGN = 128
TILE_GROUP = 4
MAP_GROUP = 4
RAY_GROUP = 2
SHARES = 4
MAP_LEAD = 1


def kernel_tables(side):
    indices = np.arange(side)
    offset = (indices[:, None] - indices[None, :]).astype(np.float32)
    taps = np.arange(-6, 7).astype(np.float32)
    total = np.sum(np.exp(-taps * taps / np.float32(8.0)))
    inside = np.abs(offset) <= 6.0
    weight = np.where(inside, np.exp(-offset * offset / np.float32(8.0)), np.float32(0.0)) / total
    smooth = weight.astype(jnp.bfloat16)
    slope = (np.float32(6.0) * offset * weight / np.float32(4.0)).astype(jnp.bfloat16)
    return np.concatenate([smooth, slope], axis=0)


def dot_nt(a, b):
    return lax.dot_general(a, b, (((1,), (1,)), ((), ())), preferred_element_type=jnp.float32)


def hat(positions, cell, frac):
    return jnp.where(
        positions == cell, 1.0 - frac, jnp.where(positions == cell + 1, frac, 0.0)
    )


def hat_rounded(positions, cell, frac):
    here = cell.astype(jnp.float32).astype(jnp.bfloat16)
    there = (cell + 1).astype(jnp.float32).astype(jnp.bfloat16)
    low = (1.0 - frac).astype(jnp.bfloat16)
    high = frac.astype(jnp.bfloat16)
    none = jnp.zeros_like(high)
    return jnp.where(positions == here, low, jnp.where(positions == there, high, none))


def look_up(table, row_cell, col_cell, row_frac, col_frac):
    side = table.shape[0] // 2
    width = row_cell.shape[1]
    rows = lax.broadcasted_iota(jnp.int32, (table.shape[1], width), 0)
    rows = rows.astype(jnp.float32).astype(jnp.bfloat16)
    cols = lax.broadcasted_iota(jnp.int32, (side, width), 0)
    row_weight = hat_rounded(rows, row_cell, row_frac)
    col_weight = hat(cols, col_cell, col_frac)
    values = jnp.dot(table, row_weight, preferred_element_type=jnp.float32)
    along_x = jnp.sum(values[:side] * col_weight, axis=0, keepdims=True)
    along_y = jnp.sum(values[side:] * col_weight, axis=0, keepdims=True)
    return along_x, along_y


def tile_fields(tile, tables):
    side = tile.shape[0]
    part = dot_nt(tables, tile).astype(jnp.bfloat16)
    along_x = dot_nt(part[:side], tables[side:])
    along_y = dot_nt(part[side:], tables[:side])
    return jnp.concatenate([along_x, along_y], axis=0).astype(jnp.bfloat16)


def map_window(along_x, along_y, col_extra, side):
    cols = along_x.shape[1]
    here = lax.broadcasted_iota(jnp.int32, (side, cols), 0)
    there = lax.broadcasted_iota(jnp.int32, (side, cols), 1)
    pick = (there == here + col_extra).astype(jnp.float32).astype(jnp.bfloat16)
    return jnp.concatenate(
        [dot_nt(pick, along_x), dot_nt(pick, along_y)], axis=0
    ).astype(jnp.bfloat16)


def flipped(value, bit):
    return value + (1 - 2 * (value // (1 << bit) % 2)) * (1 << bit)


def routes(count):
    levels = count.bit_length() - 1
    return list(range(1, levels)) + [0], list(range(levels - 1, 0, -1)) + [0]


def place(owner, order):
    return sum((owner // (1 << b) % 2) * (1 << i) for i, b in enumerate(order))


class Copies:
    def __init__(self, send, recv):
        self.send, self.recv, self.used, self.started = send, recv, 0, []

    def start(self, src, dst, device):
        i = self.used
        self.used += 1
        copy = pltpu.make_async_remote_copy(
            src_ref=src,
            dst_ref=dst,
            send_sem=self.send.at[i],
            recv_sem=self.recv.at[i],
            device_id=device,
            device_id_type=pl.DeviceIdType.MESH,
        )
        copy.start()
        self.started.append(copy)
        return copy


def copy_counts(n, nz, planes):
    levels = n.bit_length() - 1
    remote = (nz - 1) + planes * (2 * levels + (nz - 1) + 2 + 4 * (levels - 1))
    return remote, 3 * planes + nz + 3


def body(
    n,
    nz,
    windows,
    held,
    spots,
    tables,
    unmix,
    density,
    maps,
    fine_in,
    long_in,
    fractions_in,
    deflection,
    source,
    fine,
    long,
    fractions,
    every,
    out_strips,
    strips,
    used,
    full,
    landed,
    planar,
    fields,
    spots_all,
    spots_flat,
    send,
    recv,
    local,
):
    me, mz = lax.axis_index("rays"), lax.axis_index("planes")
    planes, tiles_here = density.shape[0], density.shape[1]
    part = tiles_here // 2
    levels = n.bit_length() - 1
    orders = routes(n)
    core = me % 2
    rows = used.shape[1]
    half = rows // 2
    blocks = windows.shape[2]
    side = tables.shape[1]
    width = fine_in.shape[2] // blocks
    keep = pl.multiple_of(core * half, ROW_ALIGN)
    away = pl.multiple_of((1 - core) * half, ROW_ALIGN)
    locals_used = [0]

    def local_copy(src, dst):
        copy = pltpu.make_async_copy(src, dst, local.at[locals_used[0]])
        locals_used[0] += 1
        copy.start()
        return copy

    def rays_peer(bit):
        return {"rays": flipped(me, bit), "planes": mz}

    def planes_peer(step):
        return {"rays": me, "planes": lax.rem(mz + step, nz)}

    own_spots = [place(me, order) for order in orders]
    fetched = []
    for k in range(planes):
        pair = []
        for h in range(2):
            at = (h * n + own_spots[h]) * part
            pair.append(
                local_copy(density.at[k, pl.ds(h * part, part)], every[k].at[pl.ds(at, part)])
            )
        pair.append(local_copy(maps.at[k, pl.ds(keep, half)], used.at[k, pl.ds(keep, half)]))
        fetched.append(pair)

    ray_loads = [
        local_copy(fine_in, fine),
        local_copy(long_in, long),
        local_copy(fractions_in, fractions),
    ]

    barrier = pltpu.get_barrier_semaphore()
    for bit in range(levels):
        pl.semaphore_signal(
            barrier, inc=1, device_id=rays_peer(bit), device_id_type=pl.DeviceIdType.MESH
        )
    for step in range(1, nz):
        pl.semaphore_signal(
            barrier, inc=1, device_id=planes_peer(step), device_id_type=pl.DeviceIdType.MESH
        )
    pl.semaphore_wait(barrier, levels + nz - 1)

    copies = Copies(send, recv)
    spot_copies = [
        copies.start(spots, spots_all.at[mz], planes_peer(step)) for step in range(1, nz)
    ]

    def spread_tiles(k):
        flight = []
        for i in range(levels):
            if i == 0:
                fetched[k][0].wait()
                fetched[k][1].wait()
            for copy in flight:
                copy.wait_recv()
            flight = []
            for h, order in enumerate(orders):
                base = own_spots[h] // (1 << i) * (1 << i)
                area = every[k].at[pl.ds((h * n + base) * part, part << i)]
                flight.append(copies.start(area, area, rays_peer(order[i])))
            yield
        for copy in flight:
            copy.wait_recv()
        if k == 0:
            for copy in spot_copies:
                copy.wait_recv()
            loads = [local_copy(spots, spots_flat.at[mz])]
            for step in range(1, nz):
                there = lax.rem(mz + step, nz)
                loads.append(local_copy(spots_all.at[there], spots_flat.at[there]))
            for load in loads:
                load.wait()
        flight = []
        for step in range(nz):
            there = lax.rem(mz + step, nz)

            def gather(b, carry):
                strip = every[k][spots_flat[there, k, b]]
                if step == 0:
                    strips[k, mz, b] = strip
                else:
                    out_strips[k, step - 1, b] = strip
                return carry

            lax.fori_loop(0, blocks, gather, 0)
            if step > 0:
                flight.append(
                    copies.start(out_strips.at[k, step - 1], strips.at[k, mz], planes_peer(step))
                )
        yield
        for copy in flight:
            copy.wait_recv()

    def choose(mine, here, there):
        weight = jnp.full((1, here.shape[1]), mine, jnp.float32)
        return here * weight.astype(here.dtype) + there * (1.0 - weight).astype(here.dtype)

    def spread_map(k):
        first = copies.start(maps.at[k, pl.ds(away, half)], landed.at[k, pl.ds(0, half)], rays_peer(0))
        yield
        first.wait_recv()
        fetched[k][2].wait()
        used[k, pl.ds(keep, half)] = choose(
            held[k, 0, 0], used[k, pl.ds(keep, half)], landed[k, pl.ds(0, half)]
        )
        base = [core * half + h * (half // 2) for h in range(2)]
        spot = [half + h * (half // 2) for h in range(2)]
        size = half // 2
        paths = [order[:-1] for order in orders]
        for i in range(levels - 1):
            size //= 2
            flight = []
            for h in range(2):
                bit = me // (1 << paths[h][i]) % 2
                give = pl.multiple_of(base[h] + (1 - bit) * size, ROW_ALIGN)
                flight.append(
                    copies.start(
                        used.at[k, pl.ds(give, size)],
                        landed.at[k, pl.ds(spot[h], size)],
                        rays_peer(paths[h][i]),
                    )
                )
                base[h] = base[h] + bit * size
            yield
            for h in range(2):
                flight[h].wait_recv()
                at = pl.multiple_of(base[h], ROW_ALIGN)
                total = choose(
                    held[k, h, i + 1], used[k, pl.ds(at, size)], landed[k, pl.ds(spot[h], size)]
                )
                if i < levels - 2:
                    used[k, pl.ds(at, size)] = total
                else:
                    full[k][pl.ds(at, size)] = total
                spot[h] += size
        for i in reversed(range(levels - 1)):
            flight = []
            for h in range(2):
                area = full[k].at[pl.ds(pl.multiple_of(base[h], ROW_ALIGN), size)]
                flight.append(copies.start(area, area, rays_peer(paths[h][i])))
                base[h] = base[h] - (me // (1 << paths[h][i]) % 2) * size
            yield
            size *= 2
            for copy in flight:
                copy.wait_recv()
        area = full[k].at[pl.ds(keep, half)]
        last = copies.start(area, area, rays_peer(0))
        yield
        last.wait_recv()

    chunks = map_side_chunks(rows, side)
    map_rows = rows // (2 * chunks)

    def convolve_tiles(k):
        def some(g, carry):
            made = []
            for u in range(TILE_GROUP):
                tile = strips[k, :, g * TILE_GROUP + u].reshape(side, side)
                made.append(tile_fields(tile, tables[...]))
            for u in range(TILE_GROUP):
                fields[k, g * TILE_GROUP + u] = made[u]
            return carry

        lax.fori_loop(0, blocks // TILE_GROUP, some, 0)

    def separate(k):
        kinds = 2 * chunks
        span = side // kinds

        def some(g, carry):
            parts = []
            for u in range(MAP_GROUP):
                at = pl.multiple_of((g * MAP_GROUP + u) * side, side)
                parts.append(
                    jnp.dot(
                        unmix[...], full[k][pl.ds(at, side)], preferred_element_type=jnp.float32
                    ).astype(jnp.bfloat16)
                )
            moved = jnp.concatenate(
                [part.reshape(kinds, span, side) for part in parts], axis=1
            )
            at = pl.multiple_of(g * (MAP_GROUP * span), MAP_GROUP * span)
            for j in range(kinds):
                planar[k, pl.ds(j * map_rows + at, MAP_GROUP * span)] = moved[j]
            return carry

        lax.fori_loop(0, rows // (side * MAP_GROUP), some, 0)

    def look(k, b):
        rays = pl.ds(pl.multiple_of(b * width, width), width)
        span = side + ROW_ALIGN
        pieces = []
        for comp in range(2):
            lanes = []
            for j in range(2):
                at = windows[k, 0, b] * ROW_ALIGN + (2 * j + comp) * map_rows
                lanes.append(planar[k, pl.ds(at, span)])
            pieces.append(jnp.concatenate(lanes, axis=1))
        window = map_window(pieces[0], pieces[1], windows[k, 2, b], side)
        row_extra = windows[k, 1, b]
        frac = fractions[k, :, rays]
        shift = jnp.zeros_like(frac[0:2])
        for j in range(k):
            shift = shift - ((k - j) / k) * deflection[j, :, rays]
        shift_x, shift_y = shift[0:1], shift[1:2]
        fine_cell, long_cell = fine[k, :, rays], long[k, :, rays]
        fine_x, fine_y = look_up(
            fields[k, b], fine_cell[0:1], fine_cell[1:2], frac[0:1] + shift_x, frac[1:2] + shift_y
        )
        long_x, long_y = look_up(
            window,
            long_cell[0:1] + row_extra,
            long_cell[1:2],
            frac[2:3] + shift_x / RATIO,
            frac[3:4] + shift_y / RATIO,
        )
        value = jnp.concatenate([fine_x + long_x, fine_y + long_y], axis=0)
        total = jnp.zeros_like(value)
        if k == planes - 1:
            for j in range(k):
                total = total - ((planes - j) / planes) * deflection[j, :, rays]
            total = total - (1 / planes) * value
        return rays, value, total

    def compute(k, share):
        if k == 0 and share == 0:
            for load in ray_loads:
                load.wait()
        groups = blocks // RAY_GROUP // SHARES

        def some(g, carry):
            done = [look(k, g * RAY_GROUP + u) for u in range(RAY_GROUP)]
            for rays, value, total in done:
                deflection[k, :, rays] = value
                if k == planes - 1:
                    source[:, rays] = total
            return carry

        lax.fori_loop(share * groups, (share + 1) * groups, some, 0)

    chains = {}
    for k in range(planes):
        chains[k, 0] = (max(0, k - MAP_LEAD), spread_map(k), separate)
        chains[k, 1] = (k, spread_tiles(k), convolve_tiles)
    jobs, left, moment = [], [2] * planes, 0
    while chains:
        for key in list(chains):
            begin, steps, after = chains[key]
            if moment >= begin and next(steps, True) is True:
                del chains[key]
                jobs.append(functools.partial(after, key[0]))
                left[key[0]] -= 1
                if left[key[0]] == 0:
                    jobs += [functools.partial(compute, key[0], i) for i in range(SHARES)]
            if jobs:
                jobs.pop(0)()
        moment += 1
    for job in jobs:
        job()
    for copy in copies.started:
        copy.wait_send()


def map_side_chunks(rows, side):
    chunks = 1
    while 2 * chunks * chunks * side < rows:
        chunks += 1
    return chunks


def per_device(
    n,
    nz,
    tile_density,
    long_maps,
    map_owner,
    tile_lists,
    block_slots,
    block_windows,
    fine_cells,
    long_cells,
    fractions,
):
    my_row = lax.axis_index("rays")
    planes, tiles_here, strip_rows, side = tile_density.shape
    map_side = long_maps.shape[2]
    rays_here = fine_cells.shape[2]
    blocks = block_slots.shape[1]
    part = tiles_here // 2
    chunks = map_side // COL_ALIGN
    map_rows = 2 * chunks * map_side
    tables = jnp.asarray(kernel_tables(side))

    lists = lax.dynamic_index_in_dim(tile_lists, my_row, 0, keepdims=False)
    picked = block_slots[:, :, None] == jnp.arange(lists.shape[1], dtype=jnp.int32)
    tiles = jnp.sum(jnp.where(picked, lists[:, None, :], 0), axis=2)
    owner, inside = tiles // tiles_here, tiles % tiles_here
    order_a, order_b = routes(n)
    spot_a = place(owner, order_a) * part + inside
    spot_b = (n + place(owner, order_b)) * part + inside - part
    spots = jnp.where(inside < part, spot_a, spot_b)
    spots = jnp.pad(spots, ((0, 8 - planes), (0, 128 - blocks)))
    row_at, col_at = block_windows[:, 0], block_windows[:, 1]
    row_base = jnp.minimum(row_at // ROW_ALIGN, (map_side - side) // ROW_ALIGN - 1)
    col_base = jnp.minimum(col_at // COL_ALIGN, chunks - 2)
    windows = jnp.stack(
        [
            row_base + 2 * col_base * (map_side // ROW_ALIGN),
            row_at - row_base * ROW_ALIGN,
            col_at - col_base * COL_ALIGN,
        ],
        axis=1,
    )

    own = long_maps[0].reshape(planes, map_side, 2, chunks, COL_ALIGN)
    own = jnp.transpose(own, (0, 1, 3, 2, 4)).reshape(planes, map_rows, COL_ALIGN)
    unlike = map_owner[:, None, None] ^ my_row
    levels = n.bit_length() - 1
    reached = [
        [sum(1 << b for b in ([0] + order[:-1])[:i]) for i in range(levels)]
        for order in (order_a, order_b)
    ]
    apart = jnp.asarray([[n - 1 - r for r in row] for row in reached], jnp.int32)
    held = ((unlike & apart) == 0).astype(jnp.float32)
    kinds = 2 * chunks
    span = side // kinds
    to = np.arange(side)
    unmix = (to[None, :] == (to[:, None] % span) * kinds + to[:, None] // span).astype(jnp.bfloat16)

    remote, local = copy_counts(n, nz, planes)
    vmem = pl.BlockSpec(memory_space=pltpu.VMEM)
    smem = pl.BlockSpec(memory_space=pltpu.SMEM)
    anywhere = pl.BlockSpec(memory_space=pl.ANY)
    kind = tile_density.dtype
    return pl.pallas_call(
        functools.partial(body, n, nz),
        out_shape=[
            jax.ShapeDtypeStruct((planes, 2, rays_here), jnp.float32),
            jax.ShapeDtypeStruct((2, rays_here), jnp.float32),
        ],
        in_specs=[smem, smem, vmem, vmem, vmem, anywhere, anywhere, anywhere, anywhere, anywhere],
        out_specs=[vmem, vmem],
        scratch_shapes=[
            pltpu.VMEM(fine_cells.shape, fine_cells.dtype),
            pltpu.VMEM(long_cells.shape, long_cells.dtype),
            pltpu.VMEM(fractions.shape, fractions.dtype),
            [pltpu.VMEM((n * tiles_here, strip_rows, side), kind)] * planes,
            pltpu.VMEM((planes, nz - 1, blocks, strip_rows, side), kind),
            pltpu.VMEM((planes, nz, blocks, strip_rows, side), kind),
            pltpu.VMEM((planes, map_rows, COL_ALIGN), kind),
            [pltpu.VMEM((map_rows, COL_ALIGN), kind)] * planes,
            pltpu.VMEM((planes, map_rows, COL_ALIGN), kind),
            pltpu.VMEM((planes, map_rows, COL_ALIGN), kind),
            pltpu.VMEM((planes, blocks, 2 * side, side), kind),
            pltpu.VMEM((nz,) + spots.shape, jnp.int32),
            pltpu.SMEM((nz,) + spots.shape, jnp.int32),
            pltpu.SemaphoreType.DMA((remote,)),
            pltpu.SemaphoreType.DMA((remote,)),
            pltpu.SemaphoreType.DMA((local,)),
        ],
        compiler_params=pltpu.CompilerParams(
            collective_id=0, has_side_effects=True, vmem_limit_bytes=52 * 1024 * 1024
        ),
        cost_estimate=pl.CostEstimate(
            flops=6 * planes * rays_here * 128 * 256, bytes_accessed=16 << 20, transcendentals=0
        ),
    )(windows, held, spots, tables, jnp.asarray(unmix), tile_density, own, fine_cells, long_cells, fractions)


def solution(mesh):
    return jax.shard_map(
        functools.partial(per_device, mesh.shape["rays"], mesh.shape["planes"]),
        mesh=mesh,
        in_specs=(
            P(None, "rays", "planes", None),
            P("rays", None, None, None, None),
            P(),
            P(),
            P(None, ("rays", "planes")),
            P(None, None, ("rays", "planes")),
            P(None, None, ("rays", "planes")),
            P(None, None, ("rays", "planes")),
            P(None, None, ("rays", "planes")),
        ),
        out_specs=(P(None, None, ("rays", "planes")), P(None, ("rays", "planes"))),
        check_vma=False,
    )
```

```python
import functools

import jax
import jax.numpy as jnp
import numpy as np
from jax import lax
from jax.experimental import pallas as pl
from jax.experimental.pallas import tpu as pltpu
from jax.sharding import PartitionSpec as P

RATIO = 16
ROW_ALIGN = 16
COL_ALIGN = 128
TILE_GROUP = 4
MAP_GROUP = 4
RAY_GROUP = 2
SHARES = 4
PAIR = 2
PAIR_GAP = 2


def kernel_tables(side):
    indices = np.arange(side)
    offset = (indices[:, None] - indices[None, :]).astype(np.float32)
    taps = np.arange(-6, 7).astype(np.float32)
    total = np.sum(np.exp(-taps * taps / np.float32(8.0)))
    inside = np.abs(offset) <= 6.0
    weight = np.where(inside, np.exp(-offset * offset / np.float32(8.0)), np.float32(0.0)) / total
    smooth = weight.astype(jnp.bfloat16)
    slope = (np.float32(6.0) * offset * weight / np.float32(4.0)).astype(jnp.bfloat16)
    return np.concatenate([smooth, slope], axis=0)


def dot_nt(a, b):
    return lax.dot_general(a, b, (((1,), (1,)), ((), ())), preferred_element_type=jnp.float32)


def hat(positions, cell, frac):
    return jnp.where(
        positions == cell, 1.0 - frac, jnp.where(positions == cell + 1, frac, 0.0)
    )


def hat_rounded(positions, cell, frac):
    here = cell.astype(jnp.float32).astype(jnp.bfloat16)
    there = (cell + 1).astype(jnp.float32).astype(jnp.bfloat16)
    low = (1.0 - frac).astype(jnp.bfloat16)
    high = frac.astype(jnp.bfloat16)
    none = jnp.zeros_like(high)
    return jnp.where(positions == here, low, jnp.where(positions == there, high, none))


def look_up(table, row_cell, col_cell, row_frac, col_frac):
    side = table.shape[0] // 2
    width = row_cell.shape[1]
    rows = lax.broadcasted_iota(jnp.int32, (table.shape[1], width), 0)
    rows = rows.astype(jnp.float32).astype(jnp.bfloat16)
    cols = lax.broadcasted_iota(jnp.int32, (side, width), 0)
    row_weight = hat_rounded(rows, row_cell, row_frac)
    col_weight = hat(cols, col_cell, col_frac)
    values = jnp.dot(table, row_weight, preferred_element_type=jnp.float32)
    along_x = jnp.sum(values[:side] * col_weight, axis=0, keepdims=True)
    along_y = jnp.sum(values[side:] * col_weight, axis=0, keepdims=True)
    return along_x, along_y


def tile_fields(tile, tables):
    side = tile.shape[0]
    part = dot_nt(tables, tile).astype(jnp.bfloat16)
    along_x = dot_nt(part[:side], tables[side:])
    along_y = dot_nt(part[side:], tables[:side])
    return jnp.concatenate([along_x, along_y], axis=0).astype(jnp.bfloat16)


def map_window(along_x, along_y, col_extra, side):
    cols = along_x.shape[1]
    here = lax.broadcasted_iota(jnp.int32, (side, cols), 0)
    there = lax.broadcasted_iota(jnp.int32, (side, cols), 1)
    pick = (there == here + col_extra).astype(jnp.float32).astype(jnp.bfloat16)
    return jnp.concatenate(
        [dot_nt(pick, along_x), dot_nt(pick, along_y)], axis=0
    ).astype(jnp.bfloat16)


def flipped(value, bit):
    return value + (1 - 2 * (value // (1 << bit) % 2)) * (1 << bit)


def routes(count):
    levels = count.bit_length() - 1
    return list(range(1, levels)) + [0], list(range(levels - 1, 0, -1)) + [0]


def place(owner, order):
    return sum((owner // (1 << b) % 2) * (1 << i) for i, b in enumerate(order))


class Copies:
    def __init__(self, send, recv):
        self.send, self.recv, self.used, self.started = send, recv, 0, []

    def start(self, src, dst, device):
        i = self.used
        self.used += 1
        copy = pltpu.make_async_remote_copy(
            src_ref=src,
            dst_ref=dst,
            send_sem=self.send.at[i],
            recv_sem=self.recv.at[i],
            device_id=device,
            device_id_type=pl.DeviceIdType.MESH,
        )
        copy.start()
        self.started.append(copy)
        return copy


def copy_counts(n, nz, planes):
    levels = n.bit_length() - 1
    remote = (nz - 1) + planes * (2 * levels + (nz - 1) + 2 + 4 * (levels - 1))
    return remote, 3 * planes + nz + 3


def body(
    n,
    nz,
    windows,
    owners,
    spots,
    tables,
    unmix,
    density,
    maps,
    fine_in,
    long_in,
    fractions_in,
    deflection,
    source,
    fine,
    long,
    fractions,
    every,
    out_strips,
    strips,
    used,
    full,
    landed,
    planar,
    fields,
    spots_all,
    spots_flat,
    send,
    recv,
    local,
):
    me, mz = lax.axis_index("rays"), lax.axis_index("planes")
    planes, tiles_here = density.shape[0], density.shape[1]
    part = tiles_here // 2
    levels = n.bit_length() - 1
    orders = routes(n)
    core = me % 2
    rows = used.shape[1]
    half = rows // 2
    blocks = windows.shape[2]
    side = tables.shape[1]
    width = fine_in.shape[2] // blocks
    keep = pl.multiple_of(core * half, ROW_ALIGN)
    away = pl.multiple_of((1 - core) * half, ROW_ALIGN)
    locals_used = [0]

    def local_copy(src, dst):
        copy = pltpu.make_async_copy(src, dst, local.at[locals_used[0]])
        locals_used[0] += 1
        copy.start()
        return copy

    def rays_peer(bit):
        return {"rays": flipped(me, bit), "planes": mz}

    def planes_peer(step):
        return {"rays": me, "planes": lax.rem(mz + step, nz)}

    own_spots = [place(me, order) for order in orders]
    fetched = []
    for k in range(planes):
        pair = []
        for h in range(2):
            at = (h * n + own_spots[h]) * part
            pair.append(
                local_copy(density.at[k, pl.ds(h * part, part)], every[k].at[pl.ds(at, part)])
            )
        pair.append(local_copy(maps.at[k, pl.ds(keep, half)], used.at[k, pl.ds(keep, half)]))
        fetched.append(pair)

    ray_loads = [
        local_copy(fine_in, fine),
        local_copy(long_in, long),
        local_copy(fractions_in, fractions),
    ]

    barrier = pltpu.get_barrier_semaphore()
    for bit in range(levels):
        pl.semaphore_signal(
            barrier, inc=1, device_id=rays_peer(bit), device_id_type=pl.DeviceIdType.MESH
        )
    for step in range(1, nz):
        pl.semaphore_signal(
            barrier, inc=1, device_id=planes_peer(step), device_id_type=pl.DeviceIdType.MESH
        )
    pl.semaphore_wait(barrier, levels + nz - 1)

    copies = Copies(send, recv)
    spot_copies = [
        copies.start(spots, spots_all.at[mz], planes_peer(step)) for step in range(1, nz)
    ]

    def spread_tiles(k):
        flight = []
        for i in range(levels):
            if i == 0:
                fetched[k][0].wait()
                fetched[k][1].wait()
            for copy in flight:
                copy.wait_recv()
            flight = []
            for h, order in enumerate(orders):
                base = own_spots[h] // (1 << i) * (1 << i)
                area = every[k].at[pl.ds((h * n + base) * part, part << i)]
                flight.append(copies.start(area, area, rays_peer(order[i])))
            yield
        for copy in flight:
            copy.wait_recv()
        if k == 0:
            for copy in spot_copies:
                copy.wait_recv()
            loads = [local_copy(spots, spots_flat.at[mz])]
            for step in range(1, nz):
                there = lax.rem(mz + step, nz)
                loads.append(local_copy(spots_all.at[there], spots_flat.at[there]))
            for load in loads:
                load.wait()
        flight = []
        for step in range(nz):
            there = lax.rem(mz + step, nz)

            def gather(b, carry):
                strip = every[k][spots_flat[there, k, b]]
                if step == 0:
                    strips[k, mz, b] = strip
                else:
                    out_strips[k, step - 1, b] = strip
                return carry

            lax.fori_loop(0, blocks, gather, 0)
            if step > 0:
                flight.append(
                    copies.start(out_strips.at[k, step - 1], strips.at[k, mz], planes_peer(step))
                )
        yield
        for copy in flight:
            copy.wait_recv()

    def choose(k, done, here, there):
        apart = n - 1 - sum(1 << bit for bit in done)
        unlike = jnp.bitwise_and(jnp.bitwise_xor(owners[k], me), apart)
        weight = jnp.where(jnp.full((1, here.shape[1]), unlike) == 0, 1.0, 0.0)
        return here * weight.astype(here.dtype) + there * (1.0 - weight).astype(here.dtype)

    def spread_map(k):
        first = copies.start(maps.at[k, pl.ds(away, half)], landed.at[k, pl.ds(0, half)], rays_peer(0))
        yield
        first.wait_recv()
        fetched[k][2].wait()
        used[k, pl.ds(keep, half)] = choose(
            k, [], used[k, pl.ds(keep, half)], landed[k, pl.ds(0, half)]
        )
        base = [core * half + h * (half // 2) for h in range(2)]
        spot = [half + h * (half // 2) for h in range(2)]
        size = half // 2
        paths = [order[:-1] for order in orders]
        for i in range(levels - 1):
            size //= 2
            flight = []
            for h in range(2):
                bit = me // (1 << paths[h][i]) % 2
                give = pl.multiple_of(base[h] + (1 - bit) * size, ROW_ALIGN)
                flight.append(
                    copies.start(
                        used.at[k, pl.ds(give, size)],
                        landed.at[k, pl.ds(spot[h], size)],
                        rays_peer(paths[h][i]),
                    )
                )
                base[h] = base[h] + bit * size
            yield
            for h in range(2):
                flight[h].wait_recv()
                at = pl.multiple_of(base[h], ROW_ALIGN)
                total = choose(
                    k, [0] + paths[h][:i], used[k, pl.ds(at, size)], landed[k, pl.ds(spot[h], size)]
                )
                if i < levels - 2:
                    used[k, pl.ds(at, size)] = total
                else:
                    full[k][pl.ds(at, size)] = total
                spot[h] += size
        for i in reversed(range(levels - 1)):
            flight = []
            for h in range(2):
                area = full[k].at[pl.ds(pl.multiple_of(base[h], ROW_ALIGN), size)]
                flight.append(copies.start(area, area, rays_peer(paths[h][i])))
                base[h] = base[h] - (me // (1 << paths[h][i]) % 2) * size
            yield
            size *= 2
            for copy in flight:
                copy.wait_recv()
        area = full[k].at[pl.ds(keep, half)]
        last = copies.start(area, area, rays_peer(0))
        yield
        last.wait_recv()

    chunks = map_side_chunks(rows, side)
    map_rows = rows // (2 * chunks)

    def convolve_tiles(k):
        def some(g, carry):
            made = []
            for u in range(TILE_GROUP):
                tile = strips[k, :, g * TILE_GROUP + u].reshape(side, side)
                made.append(tile_fields(tile, tables[...]))
            for u in range(TILE_GROUP):
                fields[k, g * TILE_GROUP + u] = made[u]
            return carry

        lax.fori_loop(0, blocks // TILE_GROUP, some, 0)

    def separate(k):
        kinds = 2 * chunks
        span = side // kinds

        def some(g, carry):
            parts = []
            for u in range(MAP_GROUP):
                at = pl.multiple_of((g * MAP_GROUP + u) * side, side)
                parts.append(
                    jnp.dot(
                        unmix[...], full[k][pl.ds(at, side)], preferred_element_type=jnp.float32
                    ).astype(jnp.bfloat16)
                )
            moved = jnp.concatenate(
                [part.reshape(kinds, span, side) for part in parts], axis=1
            )
            at = pl.multiple_of(g * (MAP_GROUP * span), MAP_GROUP * span)
            for j in range(kinds):
                planar[k, pl.ds(j * map_rows + at, MAP_GROUP * span)] = moved[j]
            return carry

        lax.fori_loop(0, rows // (side * MAP_GROUP), some, 0)

    def look(k, b):
        rays = pl.ds(pl.multiple_of(b * width, width), width)
        span = side + ROW_ALIGN
        pieces = []
        for comp in range(2):
            lanes = []
            for j in range(2):
                at = windows[k, 0, b] * ROW_ALIGN + (2 * j + comp) * map_rows
                lanes.append(planar[k, pl.ds(at, span)])
            pieces.append(jnp.concatenate(lanes, axis=1))
        window = map_window(pieces[0], pieces[1], windows[k, 2, b], side)
        row_extra = windows[k, 1, b]
        frac = fractions[k, :, rays]
        shift = jnp.zeros_like(frac[0:2])
        for j in range(k):
            shift = shift - ((k - j) / k) * deflection[j, :, rays]
        shift_x, shift_y = shift[0:1], shift[1:2]
        fine_cell, long_cell = fine[k, :, rays], long[k, :, rays]
        fine_x, fine_y = look_up(
            fields[k, b], fine_cell[0:1], fine_cell[1:2], frac[0:1] + shift_x, frac[1:2] + shift_y
        )
        long_x, long_y = look_up(
            window,
            long_cell[0:1] + row_extra,
            long_cell[1:2],
            frac[2:3] + shift_x / RATIO,
            frac[3:4] + shift_y / RATIO,
        )
        value = jnp.concatenate([fine_x + long_x, fine_y + long_y], axis=0)
        total = jnp.zeros_like(value)
        if k == planes - 1:
            for j in range(k):
                total = total - ((planes - j) / planes) * deflection[j, :, rays]
            total = total - (1 / planes) * value
        return rays, value, total

    def compute(k, share):
        if k == 0 and share == 0:
            for load in ray_loads:
                load.wait()
        groups = blocks // RAY_GROUP // SHARES

        def some(g, carry):
            done = [look(k, g * RAY_GROUP + u) for u in range(RAY_GROUP)]
            for rays, value, total in done:
                deflection[k, :, rays] = value
                if k == planes - 1:
                    source[:, rays] = total
            return carry

        lax.fori_loop(share * groups, (share + 1) * groups, some, 0)

    chains = {}
    for k in range(planes):
        begin = k // PAIR * PAIR_GAP
        chains[k, 0] = (begin, spread_tiles(k), convolve_tiles)
        chains[k, 1] = (begin, spread_map(k), separate)
    jobs, left, moment = [], [2] * planes, 0
    while chains:
        for key in list(chains):
            begin, steps, after = chains[key]
            if moment >= begin and next(steps, True) is True:
                del chains[key]
                jobs.append(functools.partial(after, key[0]))
                left[key[0]] -= 1
                if left[key[0]] == 0:
                    jobs += [functools.partial(compute, key[0], i) for i in range(SHARES)]
            if jobs:
                jobs.pop(0)()
        moment += 1
    for job in jobs:
        job()
    for copy in copies.started:
        copy.wait_send()


def map_side_chunks(rows, side):
    chunks = 1
    while 2 * chunks * chunks * side < rows:
        chunks += 1
    return chunks


def per_device(
    n,
    nz,
    tile_density,
    long_maps,
    map_owner,
    tile_lists,
    block_slots,
    block_windows,
    fine_cells,
    long_cells,
    fractions,
):
    my_row = lax.axis_index("rays")
    planes, tiles_here, strip_rows, side = tile_density.shape
    map_side = long_maps.shape[2]
    rays_here = fine_cells.shape[2]
    blocks = block_slots.shape[1]
    part = tiles_here // 2
    chunks = map_side // COL_ALIGN
    map_rows = 2 * chunks * map_side
    tables = jnp.asarray(kernel_tables(side))

    lists = lax.dynamic_index_in_dim(tile_lists, my_row, 0, keepdims=False)
    picked = block_slots[:, :, None] == jnp.arange(lists.shape[1], dtype=jnp.int32)
    tiles = jnp.sum(jnp.where(picked, lists[:, None, :], 0), axis=2)
    owner, inside = tiles // tiles_here, tiles % tiles_here
    order_a, order_b = routes(n)
    spot_a = place(owner, order_a) * part + inside
    spot_b = (n + place(owner, order_b)) * part + inside - part
    spots = jnp.where(inside < part, spot_a, spot_b)
    spots = jnp.pad(spots, ((0, 8 - planes), (0, 128 - blocks)))
    row_at, col_at = block_windows[:, 0], block_windows[:, 1]
    row_base = jnp.minimum(row_at // ROW_ALIGN, (map_side - side) // ROW_ALIGN - 1)
    col_base = jnp.minimum(col_at // COL_ALIGN, chunks - 2)
    windows = jnp.stack(
        [
            row_base + 2 * col_base * (map_side // ROW_ALIGN),
            row_at - row_base * ROW_ALIGN,
            col_at - col_base * COL_ALIGN,
        ],
        axis=1,
    )

    own = long_maps[0].reshape(planes, map_side, 2, chunks, COL_ALIGN)
    own = jnp.transpose(own, (0, 1, 3, 2, 4)).reshape(planes, map_rows, COL_ALIGN)
    kinds = 2 * chunks
    span = side // kinds
    to = np.arange(side)
    unmix = (to[None, :] == (to[:, None] % span) * kinds + to[:, None] // span).astype(jnp.bfloat16)

    remote, local = copy_counts(n, nz, planes)
    vmem = pl.BlockSpec(memory_space=pltpu.VMEM)
    smem = pl.BlockSpec(memory_space=pltpu.SMEM)
    anywhere = pl.BlockSpec(memory_space=pl.ANY)
    kind = tile_density.dtype
    return pl.pallas_call(
        functools.partial(body, n, nz),
        out_shape=[
            jax.ShapeDtypeStruct((planes, 2, rays_here), jnp.float32),
            jax.ShapeDtypeStruct((2, rays_here), jnp.float32),
        ],
        in_specs=[smem, smem, vmem, vmem, vmem, anywhere, anywhere, anywhere, anywhere, anywhere],
        out_specs=[vmem, vmem],
        scratch_shapes=[
            pltpu.VMEM(fine_cells.shape, fine_cells.dtype),
            pltpu.VMEM(long_cells.shape, long_cells.dtype),
            pltpu.VMEM(fractions.shape, fractions.dtype),
            [pltpu.VMEM((n * tiles_here, strip_rows, side), kind)] * planes,
            pltpu.VMEM((planes, nz - 1, blocks, strip_rows, side), kind),
            pltpu.VMEM((planes, nz, blocks, strip_rows, side), kind),
            pltpu.VMEM((planes, map_rows, COL_ALIGN), kind),
            [pltpu.VMEM((map_rows, COL_ALIGN), kind)] * planes,
            pltpu.VMEM((planes, map_rows, COL_ALIGN), kind),
            pltpu.VMEM((planes, map_rows, COL_ALIGN), kind),
            pltpu.VMEM((planes, blocks, 2 * side, side), kind),
            pltpu.VMEM((nz,) + spots.shape, jnp.int32),
            pltpu.SMEM((nz,) + spots.shape, jnp.int32),
            pltpu.SemaphoreType.DMA((remote,)),
            pltpu.SemaphoreType.DMA((remote,)),
            pltpu.SemaphoreType.DMA((local,)),
        ],
        compiler_params=pltpu.CompilerParams(
            collective_id=0, has_side_effects=True, vmem_limit_bytes=62 * 1024 * 1024
        ),
        cost_estimate=pl.CostEstimate(
            flops=6 * planes * rays_here * 128 * 256, bytes_accessed=16 << 20, transcendentals=0
        ),
    )(windows, map_owner, spots, tables, jnp.asarray(unmix), tile_density, own, fine_cells, long_cells, fractions)


def solution(mesh):
    return jax.shard_map(
        functools.partial(per_device, mesh.shape["rays"], mesh.shape["planes"]),
        mesh=mesh,
        in_specs=(
            P(None, "rays", "planes", None),
            P("rays", None, None, None, None),
            P(),
            P(),
            P(None, ("rays", "planes")),
            P(None, None, ("rays", "planes")),
            P(None, None, ("rays", "planes")),
            P(None, None, ("rays", "planes")),
            P(None, None, ("rays", "planes")),
        ),
        out_specs=(P(None, None, ("rays", "planes")), P(None, ("rays", "planes"))),
        check_vma=False,
    )
```

```python
import functools

import jax
import jax.numpy as jnp
import numpy as np
from jax import lax
from jax.experimental import pallas as pl
from jax.experimental.pallas import tpu as pltpu
from jax.sharding import PartitionSpec as P

RATIO = 16
ROW_ALIGN = 16
COL_ALIGN = 128
TILE_GROUP = 4
MAP_GROUP = 4
RAY_GROUP = 2
SHARES = 1


def kernel_tables(side):
    indices = np.arange(side)
    offset = (indices[:, None] - indices[None, :]).astype(np.float32)
    taps = np.arange(-6, 7).astype(np.float32)
    total = np.sum(np.exp(-taps * taps / np.float32(8.0)))
    inside = np.abs(offset) <= 6.0
    weight = np.where(inside, np.exp(-offset * offset / np.float32(8.0)), np.float32(0.0)) / total
    smooth = weight.astype(jnp.bfloat16)
    slope = (np.float32(6.0) * offset * weight / np.float32(4.0)).astype(jnp.bfloat16)
    return np.concatenate([smooth, slope], axis=0)


def dot_nt(a, b):
    return lax.dot_general(a, b, (((1,), (1,)), ((), ())), preferred_element_type=jnp.float32)


def hat(positions, cell, frac):
    return jnp.where(
        positions == cell, 1.0 - frac, jnp.where(positions == cell + 1, frac, 0.0)
    )


def hat_rounded(positions, cell, frac):
    here = cell.astype(jnp.float32).astype(jnp.bfloat16)
    there = (cell + 1).astype(jnp.float32).astype(jnp.bfloat16)
    low = (1.0 - frac).astype(jnp.bfloat16)
    high = frac.astype(jnp.bfloat16)
    none = jnp.zeros_like(high)
    return jnp.where(positions == here, low, jnp.where(positions == there, high, none))


def look_up(table, row_cell, col_cell, row_frac, col_frac):
    side = table.shape[0] // 2
    width = row_cell.shape[1]
    rows = lax.broadcasted_iota(jnp.int32, (table.shape[1], width), 0)
    rows = rows.astype(jnp.float32).astype(jnp.bfloat16)
    cols = lax.broadcasted_iota(jnp.int32, (side, width), 0)
    row_weight = hat_rounded(rows, row_cell, row_frac)
    col_weight = hat(cols, col_cell, col_frac)
    values = jnp.dot(table, row_weight, preferred_element_type=jnp.float32)
    along_x = jnp.sum(values[:side] * col_weight, axis=0, keepdims=True)
    along_y = jnp.sum(values[side:] * col_weight, axis=0, keepdims=True)
    return along_x, along_y


def tile_fields(tile, tables):
    side = tile.shape[0]
    part = dot_nt(tables, tile).astype(jnp.bfloat16)
    along_x = dot_nt(part[:side], tables[side:])
    along_y = dot_nt(part[side:], tables[:side])
    return jnp.concatenate([along_x, along_y], axis=0).astype(jnp.bfloat16)


def map_window(along_x, along_y, col_extra, side):
    cols = along_x.shape[1]
    here = lax.broadcasted_iota(jnp.int32, (side, cols), 0)
    there = lax.broadcasted_iota(jnp.int32, (side, cols), 1)
    pick = (there == here + col_extra).astype(jnp.float32).astype(jnp.bfloat16)
    return jnp.concatenate(
        [dot_nt(pick, along_x), dot_nt(pick, along_y)], axis=0
    ).astype(jnp.bfloat16)


def flipped(value, bit):
    return value + (1 - 2 * (value // (1 << bit) % 2)) * (1 << bit)


def routes(count):
    levels = count.bit_length() - 1
    return list(range(1, levels)) + [0], list(range(levels - 1, 0, -1)) + [0]


def place(owner, order):
    return sum((owner // (1 << b) % 2) * (1 << i) for i, b in enumerate(order))


class Copies:
    def __init__(self, send, recv):
        self.send, self.recv, self.used, self.started = send, recv, 0, []

    def start(self, src, dst, device):
        i = self.used
        self.used += 1
        copy = pltpu.make_async_remote_copy(
            src_ref=src,
            dst_ref=dst,
            send_sem=self.send.at[i],
            recv_sem=self.recv.at[i],
            device_id=device,
            device_id_type=pl.DeviceIdType.MESH,
        )
        copy.start()
        self.started.append(copy)
        return copy


def copy_counts(n, nz, planes):
    levels = n.bit_length() - 1
    remote = (nz - 1) + planes * (2 * levels + (nz - 1) + 2 + 4 * (levels - 1))
    return remote, 3 * planes + nz + 3


def body(
    n,
    nz,
    windows,
    owners,
    spots,
    tables,
    unmix,
    density,
    maps,
    fine_in,
    long_in,
    fractions_in,
    deflection,
    source,
    fine,
    long,
    fractions,
    every,
    out_strips,
    strips,
    used,
    full,
    landed,
    planar,
    fields,
    spots_all,
    spots_flat,
    send,
    recv,
    local,
):
    me, mz = lax.axis_index("rays"), lax.axis_index("planes")
    planes, tiles_here = density.shape[0], density.shape[1]
    part = tiles_here // 2
    levels = n.bit_length() - 1
    orders = routes(n)
    core = me % 2
    rows = used.shape[1]
    half = rows // 2
    blocks = windows.shape[2]
    side = tables.shape[1]
    width = fine_in.shape[2] // blocks
    keep = pl.multiple_of(core * half, ROW_ALIGN)
    away = pl.multiple_of((1 - core) * half, ROW_ALIGN)
    locals_used = [0]

    def local_copy(src, dst):
        copy = pltpu.make_async_copy(src, dst, local.at[locals_used[0]])
        locals_used[0] += 1
        copy.start()
        return copy

    def rays_peer(bit):
        return {"rays": flipped(me, bit), "planes": mz}

    def planes_peer(step):
        return {"rays": me, "planes": lax.rem(mz + step, nz)}

    own_spots = [place(me, order) for order in orders]
    fetched = []
    for k in range(planes):
        pair = []
        for h in range(2):
            at = (h * n + own_spots[h]) * part
            pair.append(
                local_copy(density.at[k, pl.ds(h * part, part)], every[k].at[pl.ds(at, part)])
            )
        pair.append(local_copy(maps.at[k, pl.ds(keep, half)], used.at[k, pl.ds(keep, half)]))
        fetched.append(pair)

    ray_loads = [
        local_copy(fine_in, fine),
        local_copy(long_in, long),
        local_copy(fractions_in, fractions),
    ]

    barrier = pltpu.get_barrier_semaphore()
    for bit in range(levels):
        pl.semaphore_signal(
            barrier, inc=1, device_id=rays_peer(bit), device_id_type=pl.DeviceIdType.MESH
        )
    for step in range(1, nz):
        pl.semaphore_signal(
            barrier, inc=1, device_id=planes_peer(step), device_id_type=pl.DeviceIdType.MESH
        )
    pl.semaphore_wait(barrier, levels + nz - 1)

    copies = Copies(send, recv)
    spot_copies = [
        copies.start(spots, spots_all.at[mz], planes_peer(step)) for step in range(1, nz)
    ]

    def spread_tiles(k):
        flight = []
        for i in range(levels):
            if i == 0:
                fetched[k][0].wait()
                fetched[k][1].wait()
            for copy in flight:
                copy.wait_recv()
            flight = []
            for h, order in enumerate(orders):
                base = own_spots[h] // (1 << i) * (1 << i)
                area = every[k].at[pl.ds((h * n + base) * part, part << i)]
                flight.append(copies.start(area, area, rays_peer(order[i])))
            yield
        for copy in flight:
            copy.wait_recv()
        if k == 0:
            for copy in spot_copies:
                copy.wait_recv()
            loads = [local_copy(spots, spots_flat.at[mz])]
            for step in range(1, nz):
                there = lax.rem(mz + step, nz)
                loads.append(local_copy(spots_all.at[there], spots_flat.at[there]))
            for load in loads:
                load.wait()
        flight = []
        for step in range(nz):
            there = lax.rem(mz + step, nz)

            def gather(b, carry):
                strip = every[k][spots_flat[there, k, b]]
                if step == 0:
                    strips[k, mz, b] = strip
                else:
                    out_strips[k, step - 1, b] = strip
                return carry

            lax.fori_loop(0, blocks, gather, 0)
            if step > 0:
                flight.append(
                    copies.start(out_strips.at[k, step - 1], strips.at[k, mz], planes_peer(step))
                )
        yield
        for copy in flight:
            copy.wait_recv()

    def choose(k, done, here, there):
        apart = n - 1 - sum(1 << bit for bit in done)
        unlike = jnp.bitwise_and(jnp.bitwise_xor(owners[k], me), apart)
        weight = jnp.where(jnp.full((1, here.shape[1]), unlike) == 0, 1.0, 0.0)
        return here * weight.astype(here.dtype) + there * (1.0 - weight).astype(here.dtype)

    def spread_map(k):
        first = copies.start(maps.at[k, pl.ds(away, half)], landed.at[k, pl.ds(0, half)], rays_peer(0))
        yield
        first.wait_recv()
        fetched[k][2].wait()
        used[k, pl.ds(keep, half)] = choose(
            k, [], used[k, pl.ds(keep, half)], landed[k, pl.ds(0, half)]
        )
        base = [core * half + h * (half // 2) for h in range(2)]
        spot = [half + h * (half // 2) for h in range(2)]
        size = half // 2
        paths = [order[:-1] for order in orders]
        for i in range(levels - 1):
            size //= 2
            flight = []
            for h in range(2):
                bit = me // (1 << paths[h][i]) % 2
                give = pl.multiple_of(base[h] + (1 - bit) * size, ROW_ALIGN)
                flight.append(
                    copies.start(
                        used.at[k, pl.ds(give, size)],
                        landed.at[k, pl.ds(spot[h], size)],
                        rays_peer(paths[h][i]),
                    )
                )
                base[h] = base[h] + bit * size
            yield
            for h in range(2):
                flight[h].wait_recv()
                at = pl.multiple_of(base[h], ROW_ALIGN)
                total = choose(
                    k, [0] + paths[h][:i], used[k, pl.ds(at, size)], landed[k, pl.ds(spot[h], size)]
                )
                if i < levels - 2:
                    used[k, pl.ds(at, size)] = total
                else:
                    full[k][pl.ds(at, size)] = total
                spot[h] += size
        for i in reversed(range(levels - 1)):
            flight = []
            for h in range(2):
                area = full[k].at[pl.ds(pl.multiple_of(base[h], ROW_ALIGN), size)]
                flight.append(copies.start(area, area, rays_peer(paths[h][i])))
                base[h] = base[h] - (me // (1 << paths[h][i]) % 2) * size
            yield
            size *= 2
            for copy in flight:
                copy.wait_recv()
        area = full[k].at[pl.ds(keep, half)]
        last = copies.start(area, area, rays_peer(0))
        yield
        last.wait_recv()

    chunks = map_side_chunks(rows, side)
    map_rows = rows // (2 * chunks)

    def convolve_tiles(k):
        def some(g, carry):
            made = []
            for u in range(TILE_GROUP):
                tile = strips[k, :, g * TILE_GROUP + u].reshape(side, side)
                made.append(tile_fields(tile, tables[...]))
            for u in range(TILE_GROUP):
                fields[k, g * TILE_GROUP + u] = made[u]
            return carry

        lax.fori_loop(0, blocks // TILE_GROUP, some, 0)

    def separate(k):
        kinds = 2 * chunks
        span = side // kinds

        def some(g, carry):
            parts = []
            for u in range(MAP_GROUP):
                at = pl.multiple_of((g * MAP_GROUP + u) * side, side)
                parts.append(
                    jnp.dot(
                        unmix[...], full[k][pl.ds(at, side)], preferred_element_type=jnp.float32
                    ).astype(jnp.bfloat16)
                )
            moved = jnp.concatenate(
                [part.reshape(kinds, span, side) for part in parts], axis=1
            )
            at = pl.multiple_of(g * (MAP_GROUP * span), MAP_GROUP * span)
            for j in range(kinds):
                planar[k, pl.ds(j * map_rows + at, MAP_GROUP * span)] = moved[j]
            return carry

        lax.fori_loop(0, rows // (side * MAP_GROUP), some, 0)

    def look(k, b):
        rays = pl.ds(pl.multiple_of(b * width, width), width)
        span = side + ROW_ALIGN
        pieces = []
        for comp in range(2):
            lanes = []
            for j in range(2):
                at = windows[k, 0, b] * ROW_ALIGN + (2 * j + comp) * map_rows
                lanes.append(planar[k, pl.ds(at, span)])
            pieces.append(jnp.concatenate(lanes, axis=1))
        window = map_window(pieces[0], pieces[1], windows[k, 2, b], side)
        row_extra = windows[k, 1, b]
        frac = fractions[k, :, rays]
        shift = jnp.zeros_like(frac[0:2])
        for j in range(k):
            shift = shift - ((k - j) / k) * deflection[j, :, rays]
        shift_x, shift_y = shift[0:1], shift[1:2]
        fine_cell, long_cell = fine[k, :, rays], long[k, :, rays]
        fine_x, fine_y = look_up(
            fields[k, b], fine_cell[0:1], fine_cell[1:2], frac[0:1] + shift_x, frac[1:2] + shift_y
        )
        long_x, long_y = look_up(
            window,
            long_cell[0:1] + row_extra,
            long_cell[1:2],
            frac[2:3] + shift_x / RATIO,
            frac[3:4] + shift_y / RATIO,
        )
        value = jnp.concatenate([fine_x + long_x, fine_y + long_y], axis=0)
        total = jnp.zeros_like(value)
        if k == planes - 1:
            for j in range(k):
                total = total - ((planes - j) / planes) * deflection[j, :, rays]
            total = total - (1 / planes) * value
        return rays, value, total

    def compute(k, share):
        if k == 0 and share == 0:
            for load in ray_loads:
                load.wait()
        groups = blocks // RAY_GROUP // SHARES

        def some(g, carry):
            done = [look(k, g * RAY_GROUP + u) for u in range(RAY_GROUP)]
            for rays, value, total in done:
                deflection[k, :, rays] = value
                if k == planes - 1:
                    source[:, rays] = total
            return carry

        lax.fori_loop(share * groups, (share + 1) * groups, some, 0)

    chains = {}
    for k in range(planes):
        chains[k, 0] = (k, spread_tiles(k), convolve_tiles)
        chains[k, 1] = (k, spread_map(k), separate)
    jobs, left, moment = [], [2] * planes, 0
    while chains:
        for key in list(chains):
            begin, steps, after = chains[key]
            if moment >= begin and next(steps, True) is True:
                del chains[key]
                jobs.append(functools.partial(after, key[0]))
                left[key[0]] -= 1
                if left[key[0]] == 0:
                    jobs += [functools.partial(compute, key[0], i) for i in range(SHARES)]
        for job in jobs:
            job()
        jobs = []
        moment += 1
    for copy in copies.started:
        copy.wait_send()


def map_side_chunks(rows, side):
    chunks = 1
    while 2 * chunks * chunks * side < rows:
        chunks += 1
    return chunks


def per_device(
    n,
    nz,
    tile_density,
    long_maps,
    map_owner,
    tile_lists,
    block_slots,
    block_windows,
    fine_cells,
    long_cells,
    fractions,
):
    my_row = lax.axis_index("rays")
    planes, tiles_here, strip_rows, side = tile_density.shape
    map_side = long_maps.shape[2]
    rays_here = fine_cells.shape[2]
    blocks = block_slots.shape[1]
    part = tiles_here // 2
    chunks = map_side // COL_ALIGN
    map_rows = 2 * chunks * map_side
    tables = jnp.asarray(kernel_tables(side))

    lists = lax.dynamic_index_in_dim(tile_lists, my_row, 0, keepdims=False)
    picked = block_slots[:, :, None] == jnp.arange(lists.shape[1], dtype=jnp.int32)
    tiles = jnp.sum(jnp.where(picked, lists[:, None, :], 0), axis=2)
    owner, inside = tiles // tiles_here, tiles % tiles_here
    order_a, order_b = routes(n)
    spot_a = place(owner, order_a) * part + inside
    spot_b = (n + place(owner, order_b)) * part + inside - part
    spots = jnp.where(inside < part, spot_a, spot_b)
    spots = jnp.pad(spots, ((0, 8 - planes), (0, 128 - blocks)))
    row_at, col_at = block_windows[:, 0], block_windows[:, 1]
    row_base = jnp.minimum(row_at // ROW_ALIGN, (map_side - side) // ROW_ALIGN - 1)
    col_base = jnp.minimum(col_at // COL_ALIGN, chunks - 2)
    windows = jnp.stack(
        [
            row_base + 2 * col_base * (map_side // ROW_ALIGN),
            row_at - row_base * ROW_ALIGN,
            col_at - col_base * COL_ALIGN,
        ],
        axis=1,
    )

    own = long_maps[0].reshape(planes, map_side, 2, chunks, COL_ALIGN)
    own = jnp.transpose(own, (0, 1, 3, 2, 4)).reshape(planes, map_rows, COL_ALIGN)
    kinds = 2 * chunks
    span = side // kinds
    to = np.arange(side)
    unmix = (to[None, :] == (to[:, None] % span) * kinds + to[:, None] // span).astype(jnp.bfloat16)

    remote, local = copy_counts(n, nz, planes)
    vmem = pl.BlockSpec(memory_space=pltpu.VMEM)
    smem = pl.BlockSpec(memory_space=pltpu.SMEM)
    anywhere = pl.BlockSpec(memory_space=pl.ANY)
    kind = tile_density.dtype
    return pl.pallas_call(
        functools.partial(body, n, nz),
        out_shape=[
            jax.ShapeDtypeStruct((planes, 2, rays_here), jnp.float32),
            jax.ShapeDtypeStruct((2, rays_here), jnp.float32),
        ],
        in_specs=[smem, smem, vmem, vmem, vmem, anywhere, anywhere, anywhere, anywhere, anywhere],
        out_specs=[vmem, vmem],
        scratch_shapes=[
            pltpu.VMEM(fine_cells.shape, fine_cells.dtype),
            pltpu.VMEM(long_cells.shape, long_cells.dtype),
            pltpu.VMEM(fractions.shape, fractions.dtype),
            [pltpu.VMEM((n * tiles_here, strip_rows, side), kind)] * planes,
            pltpu.VMEM((planes, nz - 1, blocks, strip_rows, side), kind),
            pltpu.VMEM((planes, nz, blocks, strip_rows, side), kind),
            pltpu.VMEM((planes, map_rows, COL_ALIGN), kind),
            [pltpu.VMEM((map_rows, COL_ALIGN), kind)] * planes,
            pltpu.VMEM((planes, map_rows, COL_ALIGN), kind),
            pltpu.VMEM((planes, map_rows, COL_ALIGN), kind),
            pltpu.VMEM((planes, blocks, 2 * side, side), kind),
            pltpu.VMEM((nz,) + spots.shape, jnp.int32),
            pltpu.SMEM((nz,) + spots.shape, jnp.int32),
            pltpu.SemaphoreType.DMA((remote,)),
            pltpu.SemaphoreType.DMA((remote,)),
            pltpu.SemaphoreType.DMA((local,)),
        ],
        compiler_params=pltpu.CompilerParams(
            collective_id=0, has_side_effects=True, vmem_limit_bytes=62 * 1024 * 1024
        ),
        cost_estimate=pl.CostEstimate(
            flops=6 * planes * rays_here * 128 * 256, bytes_accessed=16 << 20, transcendentals=0
        ),
    )(windows, map_owner, spots, tables, jnp.asarray(unmix), tile_density, own, fine_cells, long_cells, fractions)


def solution(mesh):
    return jax.shard_map(
        functools.partial(per_device, mesh.shape["rays"], mesh.shape["planes"]),
        mesh=mesh,
        in_specs=(
            P(None, "rays", "planes", None),
            P("rays", None, None, None, None),
            P(),
            P(),
            P(None, ("rays", "planes")),
            P(None, None, ("rays", "planes")),
            P(None, None, ("rays", "planes")),
            P(None, None, ("rays", "planes")),
            P(None, None, ("rays", "planes")),
        ),
        out_specs=(P(None, None, ("rays", "planes")), P(None, ("rays", "planes"))),
        check_vma=False,
    )
```
